128 devices in a mesh: dp: 2 (over x_lo), expert: 64 (over x_hi, z, y, core).
Axes of the slice: x: 4 (x_hi: 2, x_lo: 2; x = x_hi * 2 + x_lo), y: 4, z: 4, core: 2. Of those that a mesh axis runs over, the one named last changes fastest.
Arguments:
- tokens: bfloat16 [2048, 7168], P(('dp', 'expert')), may hold values from -6 to 6
- picks: int32 [2048, 8], P(('dp', 'expert')), may hold values from 0 to 63, all different within a row; in each aligned block of 16 rows (0 to 15, 16 to 31, ...) at most 4 rows name the same one
- mix_weights: float32 [2048, 8], P(('dp', 'expert')), may hold values from 0.1 to 0.6
- pairs: int32 [16, 2], replicated, may hold values from 0 to 63, as said below
- gate_weight: bfloat16 [64, 7168, 1024], P('expert', None, 'dp'), may hold values from -0.0625 to 0.0625
- up_weight: bfloat16 [64, 7168, 1024], P('expert', None, 'dp'), may hold values from -0.0625 to 0.0625
- down_weight: bfloat16 [64, 1024, 7168], P('expert', 'dp'), may hold values from -0.1875 to 0.1875
Outputs:
- combined: bfloat16 [2048, 7168], P(('dp', 'expert'))
The draws below stay inside these ranges and needn't reach their ends.
Inputs may be any that keep to these rules, and one draw needn't show every extreme that they name: `picks`: each row names 8 different slots. The rows of one device name one slot at most 4 times, and in every draw some device's rows name some slot exactly 4 times. Each row is a pair (a, a + 32) with a below 32; no position stands in two pairs; positions 0 and 31 always stand in a pair.
All inputs are finite; a program needn't handle non-finite values.
Results may differ from the reference program's by a relative error of at most 0.012.
Values may be sent and summed in bfloat16 or wider, within the bound.
No kernel may reach another device: no remote copies, remote signals or barrier semaphores. Data moves between devices by JAX's collectives and lax.ppermute only.
A program may use at most 128 MiB of HBM per device.

```python
import math
import jax
import jax.numpy as jnp
import numpy as np
from jax import lax

D = 7168
HID = 1024
TOP = 8
TOK_DEV = 16
EXPERTS = 64
CAP = 4
SWAPS = 16
TOKENS = 2048
N_DP = 2
DEVICES = 128


def draw_pairs(key, part):
    key = jax.random.fold_in(key, 11)
    first_key = jax.random.fold_in(key, 1)
    order_key = jax.random.fold_in(key, 2)
    halfway = EXPERTS // 2
    others = jax.random.permutation(first_key, jnp.arange(1, halfway - 1, dtype=jnp.int32))[:SWAPS - 2].astype(jnp.int32)
    fixed = jnp.array([0, halfway - 1], jnp.int32)
    lower = jnp.concatenate([fixed, others]).astype(jnp.int32)
    lower = jax.random.permutation(order_key, lower).astype(jnp.int32)
    return jnp.stack([lower, lower + halfway], axis=1).astype(jnp.int32)


def level_of(rng, shape, cuts, smallest, largest):
    def one(position, shards_of):
        heights = jax.random.uniform(jax.random.fold_in(jax.random.fold_in(rng, 6), position), (shards_of,), jnp.float32, smallest / len(cuts), largest / len(cuts))
        return jnp.repeat(jnp.exp(heights), shape[position] // shards_of).reshape((-1,) + (1,) * (len(shape) - position - 1))

    loudness = one(*cuts[0])
    for cut in cuts[1:]:
        loudness = loudness * one(*cut)
    return loudness


def assign_block(own_key, own, number, rows, amount, top, most, slope):
    order = jax.random.permutation(own_key, amount)
    heavy_load, usual = shares(amount, rows * top, most, slope, True), shares(amount, rows * top, most, slope, False)
    places = jnp.arange(amount)

    def named(tallies, rotation):
        used = int((tallies > 0).sum())
        fixed = max(1, used // 4)
        moved = fixed + (places - fixed + rotation * (used - fixed)) % max(1, amount - fixed)
        return jnp.zeros((amount,), jnp.int32).at[order[jnp.where(places < fixed, places, moved)]].set(jnp.asarray(tallies, jnp.int32))

    tallies = jnp.where(number % 4 == 0, named(heavy_load, number // 4), named(usual, number - number // 4 - 1))
    mixed = jax.random.permutation(jax.random.fold_in(own, 3), amount)
    giver, sink = mixed[0:amount // 2 * 2:2], mixed[1:amount // 2 * 2:2]
    margin = jnp.minimum(tallies[giver] - 1, most - tallies[sink]) // 2
    margin = jnp.where((giver == order[0]) | (sink == order[0]) | (tallies[sink] == 0), 0, jnp.maximum(margin, 0))
    moved = jax.random.randint(jax.random.fold_in(own, 4), (amount // 2,), 0, 1 << 20) % (margin + 1)
    tallies = tallies.at[giver].add(-moved).at[sink].add(moved)
    items = jnp.searchsorted(jnp.cumsum(tallies), jnp.arange(rows * top), side="right").astype(jnp.int32)
    grid = items.reshape(top, rows).T
    grid = grid[jax.random.permutation(jax.random.fold_in(own, 1), rows)]
    rotation = jax.random.randint(jax.random.fold_in(own, 2), (rows, 1), 0, top)
    return jnp.take_along_axis(grid, (jnp.arange(top)[None, :] + rotation) % top, axis=1)


def shares(number_of, total, bound, slope, full):
    portions = [(1 << 20) // math.isqrt(rank ** slope) + 1 for rank in range(1, number_of + 1)]
    largest = bound if full else min(bound, max(-(-total // number_of), total * portions[0] // sum(portions)))
    least = 1 if total - largest >= number_of - 1 else 0
    counts, spare = [largest] + [least] * (number_of - 1), total - largest - least * (number_of - 1)
    while spare > 0:
        movable = [i for i in range(1, number_of) if counts[i] < largest] or [i for i in range(1, number_of) if counts[i] < bound]
        pool, remaining = sum([portions[i] for i in movable]), spare
        for i in movable:
            addition = min(bound - counts[i], max(1, remaining * portions[i] // pool), spare)
            counts[i] = counts[i] + addition
            spare = spare - addition
    return np.array(counts)


def bell_draw(own_key, shape, width, most, shards=(), kind=jnp.bfloat16):
    values = jax.random.normal(own_key, shape, jnp.float32) * width
    if len(shards) > 0:
        values = level_of(own_key, shape, shards, -0.22, 0.18) * values
    return jnp.clip(values, min=-most, max=most).astype(kind)


def setup_inputs(seed: int = 0) -> dict:
    key_of = jax.random.split(jax.random.key(seed), 8)
    tokens = bell_draw(key_of[0], (TOKENS, D), 1.0, 6.0, ((0, 128),))
    picks_keys = jax.random.split(jax.random.fold_in(key_of[1], 1), TOKENS // TOK_DEV)
    picks_turns = jax.random.permutation(jax.random.fold_in(key_of[1], 3), TOKENS // TOK_DEV)
    picks = jax.vmap(lambda own, number: assign_block(jax.random.fold_in(key_of[1], 2), own, number, TOK_DEV, EXPERTS, TOP, CAP, 2))(picks_keys, picks_turns).reshape((TOKENS, TOP))
    mix_weights = jnp.clip(0.1 + 0.5 * jax.random.uniform(key_of[2], (TOKENS, TOP), jnp.float32) ** level_of(key_of[2], (TOKENS, TOP), ((0, 128),), -0.2, 0.2), 0.1, 0.6)
    pairs = draw_pairs(jax.random.fold_in(key_of[7], 71), 0)
    gate_weight = bell_draw(key_of[4], (EXPERTS, D, HID), D ** -0.5, 0.0625, ((0, 64), (2, 2)))
    up_weight = bell_draw(key_of[5], (EXPERTS, D, HID), D ** -0.5, 0.0625, ((0, 64), (2, 2)))
    down_weight = bell_draw(key_of[6], (EXPERTS, HID, D), HID ** -0.5, 0.1875, ((0, 64), (1, 2)))
    return {"tokens": tokens, "picks": picks, "mix_weights": mix_weights, "pairs": pairs, "gate_weight": gate_weight, "up_weight": up_weight, "down_weight": down_weight}


def expert_apply(rows, gate_w, up_w, down_w):
    gate_proj = jnp.dot(rows, gate_w, preferred_element_type=jnp.float32)
    up_proj = jnp.dot(rows, up_w, preferred_element_type=jnp.float32)
    hidden = (jax.nn.silu(gate_proj) * up_proj).astype(jnp.bfloat16)
    share = HID // N_DP
    total = jnp.zeros((rows.shape[0], D), jnp.float32)
    for half_index in range(N_DP):
        piece = jnp.dot(hidden[:, half_index * share:(half_index + 1) * share],
                        down_w[half_index * share:(half_index + 1) * share],
                        preferred_element_type=jnp.float32).astype(jnp.bfloat16)
        piece = lax.optimization_barrier(piece)
        total = total + piece.astype(jnp.float32)
    return total.astype(jnp.bfloat16)


def reference(tokens, picks, mix_weights, pairs, gate_weight, up_weight, down_weight):
    slot_ids = jnp.arange(EXPERTS, dtype=jnp.int32)
    low_hit = jnp.any(pairs[:, 0][None, :] == slot_ids[:, None], axis=1)
    high_hit = jnp.any(pairs[:, 1][None, :] == slot_ids[:, None], axis=1)
    halfway = EXPERTS // 2
    source = jnp.where(low_hit, slot_ids + halfway, jnp.where(high_hit, slot_ids - halfway, slot_ids)).astype(jnp.int32)
    flat_picks = picks.reshape(-1)
    limit = DEVICES * CAP
    places = jnp.arange(limit, dtype=jnp.int32)

    def one_expert(results, slot):
        hit = flat_picks == slot
        count = jnp.sum(hit.astype(jnp.int32))
        index = jnp.nonzero(hit, size=limit, fill_value=0)[0].astype(jnp.int32)
        valid = places < count
        rows = tokens[index // TOP]
        owner = source[slot]
        output = expert_apply(rows, gate_weight[owner], up_weight[owner], down_weight[owner])
        results = results.at[index].add(jnp.where(valid[:, None], output.astype(jnp.float32), 0.0))
        return results, None

    start = jnp.zeros((TOKENS * TOP, D), jnp.float32)
    results, unused = lax.scan(one_expert, start, slot_ids)
    picked = results.reshape(TOKENS, TOP, D)
    mixed = jnp.einsum("tkd,tk->td", picked, mix_weights.astype(jnp.float32))
    return mixed.astype(jnp.bfloat16)
```

```python
import jax
import jax.numpy as jnp
from jax import lax
from jax.sharding import Mesh, PartitionSpec as P

X_AXES = ("dp", "xh")
ZY_AXES = ("z", "y")
ALL_AXES = ("dp", "xh", "z", "y", "c")
META = 128


def other_core(value):
    return lax.ppermute(value, "c", [(0, 1), (1, 0)])


def per_device(tokens, picks, mix_weights, pairs, gate_weight, up_weight, down_weight):
    tok_rows, width = tokens.shape
    top = picks.shape[1]
    xs = lax.axis_size("dp") * lax.axis_size("xh")
    columns = lax.axis_size("z") * lax.axis_size("y")
    cores = lax.axis_size("c")
    half = lax.axis_size("xh") * columns * cores // 2
    cap = 4
    groups = cores * xs
    pooled = groups * tok_rows
    rows = columns * groups * cap

    moved = jnp.any(picks[:, :, None] == pairs.reshape(-1), axis=-1)
    owner = jnp.where(moved, picks ^ half, picks)

    mix_hi = lax.reduce_precision(mix_weights, 8, 7)
    mix_lo = mix_weights - mix_hi
    meta = jnp.concatenate([owner.astype(jnp.float32), mix_hi, mix_lo], axis=1)
    meta = jnp.pad(meta, ((0, 0), (0, META - 3 * top))).astype(jnp.bfloat16)
    packed = jnp.concatenate([tokens, meta], axis=1)
    line = lax.all_gather(packed, X_AXES, axis=0, tiled=True)
    line = jnp.concatenate([line, other_core(line)], axis=0)
    pool = line[:, :width]
    meta = line[:, width:].astype(jnp.float32)
    owner = meta[:, :top].astype(jnp.int32)
    mix_hi = meta[:, top:2 * top]
    mix_lo = meta[:, 2 * top:3 * top]

    own_xh = lax.axis_index("xh")
    own_c = lax.axis_index("c")
    column_owner = own_xh * half + jnp.arange(columns, dtype=jnp.int32) * cores + own_c
    match = owner[None, :, :] == column_owner[:, None, None]
    hit = jnp.any(match, axis=2)
    hi = jnp.sum(jnp.where(match, mix_hi[None], 0.0), axis=2)
    lo = jnp.sum(jnp.where(match, mix_lo[None], 0.0), axis=2)
    counts = hit.astype(jnp.int32).reshape(columns, groups, tok_rows)
    rank = (jnp.cumsum(counts, axis=2) - counts).reshape(columns, pooled)
    slot_group = jnp.arange(groups * cap, dtype=jnp.int32) // cap
    slot_rank = jnp.arange(groups * cap, dtype=jnp.int32) % cap
    token_group = jnp.arange(pooled, dtype=jnp.int32) // tok_rows
    place = (
        hit[:, None, :]
        & (rank[:, None, :] == slot_rank[None, :, None])
        & (slot_group[None, :, None] == token_group[None, None, :])
    )
    spread = place.astype(jnp.bfloat16).reshape(rows, pooled)
    weight_hi = jnp.where(place, hi[:, None, :], 0.0).astype(jnp.bfloat16).reshape(rows, pooled)
    weight_lo = jnp.where(place, lo[:, None, :], 0.0).astype(jnp.bfloat16).reshape(rows, pooled)

    send = jnp.dot(spread, pool, preferred_element_type=jnp.float32).astype(jnp.bfloat16)
    recv = lax.all_to_all(send, ZY_AXES, split_axis=0, concat_axis=0, tiled=True)

    gate = jnp.dot(recv, gate_weight[0], preferred_element_type=jnp.float32)
    up = jnp.dot(recv, up_weight[0], preferred_element_type=jnp.float32)
    hidden = (jax.nn.silu(gate) * up).astype(jnp.bfloat16)
    output = jnp.dot(hidden, down_weight[0], preferred_element_type=jnp.float32).astype(jnp.bfloat16)

    back = lax.all_to_all(output, ZY_AXES, split_axis=0, concat_axis=0, tiled=True)
    mixer = jnp.concatenate([weight_hi, weight_lo], axis=1)
    mixed = lax.dot_general(mixer, back, (((0,), (0,)), ((), ())), preferred_element_type=jnp.float32)
    mixed = mixed[:pooled] + mixed[pooled:]
    near = mixed[:pooled // 2]
    far = other_core(mixed[pooled // 2:].astype(jnp.bfloat16))
    part = (near + far.astype(jnp.float32)).astype(jnp.bfloat16)
    parts = lax.all_to_all(part, X_AXES, split_axis=0, concat_axis=0, tiled=True)
    parts = parts.reshape(xs, tok_rows, width).astype(jnp.float32)
    return jnp.sum(parts, axis=0).astype(jnp.bfloat16)


def solution(mesh):
    fine = Mesh(mesh.devices.reshape(2, 2, 4, 4, 2), ALL_AXES)
    expert = ("xh", "z", "y", "c")
    return jax.shard_map(
        per_device,
        mesh=fine,
        in_specs=(
            P(ALL_AXES, None),
            P(ALL_AXES, None),
            P(ALL_AXES, None),
            P(),
            P(expert, None, "dp"),
            P(expert, None, "dp"),
            P(expert, "dp", None),
        ),
        out_specs=P(ALL_AXES, None),
        check_vma=False,
    )
```

```python
import itertools

import jax
import jax.numpy as jnp
from jax import lax
from jax.sharding import Mesh, PartitionSpec as P

ALL_AXES = ("dp", "xh", "z", "y", "c")
RING = 4
CORES = 2
CAP = 4
META = 128
MAIN = 2432
SIDE = 1152
SHIFTS = (0, 1, 3, 2)


def flat_index(x, z, y, c):
    return ((((x % 2) * 2 + x // 2) * RING + z) * RING + y) * CORES + c


def ring_perm(axes, shift):
    pairs = []
    for x, z, y, c in itertools.product(range(RING), range(RING), range(RING), range(CORES)):
        there = {"x": x, "z": z, "y": y}
        there[axes[c]] = (there[axes[c]] + shift) % RING
        pairs.append((flat_index(x, z, y, c), flat_index(there["x"], there["z"], there["y"], c)))
    return pairs


def moved_along(value, axes, shift):
    return lax.ppermute(value, ALL_AXES, ring_perm(axes, shift))


def other_core(value):
    return lax.ppermute(value, "c", [(0, 1), (1, 0)])


MAIN_ROUTE = (("z", "y"), ("y", "x"), ("x", "z"))
SIDE_ROUTE = (("x", "x"), ("z", "z"), ("y", "y"))


def gathered(value, axes):
    return [value] + [moved_along(value, axes, s) for s in SHIFTS[1:]]


def scattered(blocks, axes):
    return [blocks[0]] + [moved_along(b, axes, -s % RING) for b, s in zip(blocks[1:], SHIFTS[1:])]


def plan(meta, experts, top, tok_rows, inner):
    pooled = meta.shape[0]
    groups = pooled // tok_rows
    meta = meta.astype(jnp.float32)
    owner = meta[:, :top].astype(jnp.int32)
    match = owner[None, :, :] == experts[:, None, None]
    hit = jnp.any(match, axis=2)
    hi = jnp.sum(jnp.where(match, meta[None, :, top:2 * top], 0.0), axis=2)
    lo = jnp.sum(jnp.where(match, meta[None, :, 2 * top:3 * top], 0.0), axis=2)
    token = jnp.arange(pooled, dtype=jnp.int32)
    group = token // tok_rows
    before = (group[:, None] == group[None, :]) & (token[:, None] < token[None, :])
    rank = jnp.dot(hit.astype(jnp.bfloat16), before.astype(jnp.bfloat16), preferred_element_type=jnp.float32)
    rank = rank.astype(jnp.int32)
    slot_rank = jnp.arange(groups * CAP, dtype=jnp.int32) % CAP
    slot_group = jnp.repeat(inner, CAP)
    place = (
        hit[:, None, :]
        & (rank[:, None, :] == slot_rank[None, :, None])
        & (slot_group[None, :, None] == group[None, None, :])
    )
    return place, hi, lo


def pack(place, pool):
    spread = place.astype(jnp.bfloat16).reshape(RING, -1, pool.shape[0])
    return [jnp.dot(spread[r], pool, preferred_element_type=jnp.float32).astype(jnp.bfloat16) for r in range(RING)]


def combine(place, hi, lo, blocks):
    pooled = place.shape[2]
    w_hi = jnp.where(place, hi[:, None, :], 0.0).astype(jnp.bfloat16).reshape(-1, pooled)
    w_lo = jnp.where(place, lo[:, None, :], 0.0).astype(jnp.bfloat16).reshape(-1, pooled)
    rows = jnp.concatenate(blocks, axis=0)
    dims = (((0,), (0,)), ((), ()))
    total = lax.dot_general(w_hi, rows, dims, preferred_element_type=jnp.float32)
    total = total + lax.dot_general(w_lo, rows, dims, preferred_element_type=jnp.float32)
    return total.astype(jnp.bfloat16)


def summed(blocks):
    return sum(b.astype(jnp.float32) for b in blocks).astype(jnp.bfloat16)


def split_rows(value):
    return list(value.reshape(RING, -1, value.shape[-1]))


def per_device(tokens, picks, mix_weights, pairs, gate_weight, up_weight, down_weight):
    tok_rows, width = tokens.shape
    top = picks.shape[1]
    c = lax.axis_index("c")
    x = lax.axis_index("xh") * 2 + lax.axis_index("dp")
    z = lax.axis_index("z")
    y = lax.axis_index("y")
    first = c == 0
    tail = MAIN + 2 * SIDE

    moved = jnp.any(picks[:, :, None] == pairs.reshape(-1), axis=-1)
    owner = jnp.where(moved, picks ^ 32, picks)
    mix_hi = lax.reduce_precision(mix_weights, 8, 7)
    meta = jnp.concatenate([owner.astype(jnp.float32), mix_hi, mix_weights - mix_hi], axis=1)
    meta = jnp.pad(meta, ((0, 0), (0, META - 3 * top))).astype(jnp.bfloat16)

    left = jnp.concatenate([tokens[:, :MAIN], meta, tokens[:, MAIN:MAIN + SIDE], meta], axis=1)
    right = jnp.concatenate([tokens[:, tail:], meta, tokens[:, MAIN + SIDE:tail], meta], axis=1)
    mine = jnp.where(first, left, right)
    theirs = other_core(jnp.where(first, right, left))
    both = jnp.where(first, jnp.concatenate([mine, theirs]), jnp.concatenate([theirs, mine]))
    main, side = both[:, :MAIN + META], both[:, MAIN + META:]
    for step in range(2):
        main_blocks = gathered(main, MAIN_ROUTE[step])
        side_blocks = gathered(side, SIDE_ROUTE[step])
        main = jnp.concatenate(main_blocks, axis=0)
        side = jnp.concatenate(side_blocks, axis=0)

    shifts = jnp.array(SHIFTS, jnp.int32)[:, None]
    core = jnp.stack([c, 1 - c])[None, :]
    x_main = jnp.where(first, (x + shifts) % RING, x)
    z_main = jnp.where(first, z, (z + shifts) % RING)
    main_experts = ((x_main // 2 * RING + z_main) * RING + y) * CORES + core
    side_experts = ((x // 2 * RING + z) * RING + (y + shifts) % RING) * CORES + core
    line = jnp.arange(RING * RING * CORES, dtype=jnp.int32)
    turned = line.reshape(RING, RING, CORES).swapaxes(0, 1).reshape(-1)
    main_inner = jnp.where(first, turned, line)
    main_place, main_hi, main_lo = plan(main[:, MAIN:], main_experts.reshape(-1), top, tok_rows, main_inner)
    side_place, side_hi, side_lo = plan(side[:, SIDE:], side_experts.reshape(-1), top, tok_rows, turned)

    main_out = pack(main_place, main[:, :MAIN])
    side_out = pack(side_place, side[:, :SIDE])
    main_in = [main_out[0]] + [moved_along(b, MAIN_ROUTE[2], s) for b, s in zip(main_out[1:], SHIFTS[1:])]
    side_in = [side_out[0]] + [moved_along(b, SIDE_ROUTE[2], s) for b, s in zip(side_out[1:], SHIFTS[1:])]
    half = main_in[0].shape[0] // 2
    main_keep = jnp.concatenate([b[:half] for b in main_in], axis=0)
    side_keep = jnp.concatenate([b[:half] for b in side_in], axis=0)
    main_give = other_core(jnp.concatenate([b[half:] for b in main_in], axis=0))
    side_give = other_core(jnp.concatenate([b[half:] for b in side_in], axis=0))

    a_rows = jnp.where(first, main_keep, main_give)
    b_rows = jnp.where(first, main_give, main_keep)
    s_rows = jnp.concatenate(
        [jnp.where(first, side_keep, side_give), jnp.where(first, side_give, side_keep)], axis=1)
    rows = a_rows.shape[0]

    def from_b(v):
        return v.reshape(RING, RING, -1, v.shape[-1]).swapaxes(0, 1).reshape(v.shape)

    def from_s(v):
        return v.reshape(RING, RING, RING, -1, v.shape[-1]).transpose(1, 2, 0, 3, 4).reshape(v.shape)

    def to_s(v):
        return v.reshape(RING, RING, RING, -1, v.shape[-1]).transpose(2, 0, 1, 3, 4).reshape(v.shape)

    def project(w):
        a = jnp.dot(a_rows, w[:MAIN], preferred_element_type=jnp.float32)
        b = jnp.dot(b_rows, w[tail:], preferred_element_type=jnp.float32)
        s = jnp.dot(s_rows, w[MAIN:tail], preferred_element_type=jnp.float32)
        return a + from_b(b) + from_s(s)

    gate = project(gate_weight[0])
    up = project(up_weight[0])
    hidden = (jax.nn.silu(gate) * up).astype(jnp.bfloat16)

    down = down_weight[0]
    hidden_b, hidden_s = from_b(hidden), to_s(hidden)

    def expand(h, w):
        return jnp.dot(h, w, preferred_element_type=jnp.float32).astype(jnp.bfloat16)

    out_a = expand(hidden, down[:, :MAIN])
    out_b = expand(hidden_b, down[:, tail:])
    out_s = expand(hidden_s, down[:, MAIN:tail])
    s_left, s_right = out_s[:, :SIDE], out_s[:, SIDE:]
    main_far = other_core(jnp.where(first, out_b, out_a))
    side_far = other_core(jnp.where(first, s_right, s_left))
    main_near = jnp.where(first, out_a, out_b)
    side_near = jnp.where(first, s_left, s_right)

    def back(near, far, axes):
        blocks = [jnp.concatenate(pair, axis=0) for pair in zip(split_rows(near), split_rows(far))]
        return scattered(blocks, axes)

    main_back = back(main_near, main_far, MAIN_ROUTE[2])
    side_back = back(side_near, side_far, SIDE_ROUTE[2])
    main = combine(main_place, main_hi, main_lo, main_back)
    side = combine(side_place, side_hi, side_lo, side_back)
    for step in (1, 0):
        main_blocks = scattered(split_rows(main), MAIN_ROUTE[step])
        side_blocks = scattered(split_rows(side), SIDE_ROUTE[step])
        main = summed(main_blocks)
        side = summed(side_blocks)
    done = jnp.concatenate([main, side], axis=1)
    own = jnp.where(first, done[:tok_rows], done[tok_rows:])
    rest = other_core(jnp.where(first, done[tok_rows:], done[:tok_rows]))
    lower = jnp.where(first, own, rest)
    upper = jnp.where(first, rest, own)
    return jnp.concatenate([lower, upper[:, MAIN:], upper[:, :MAIN]], axis=1)


def solution(mesh):
    fine = Mesh(mesh.devices.reshape(2, 2, RING, RING, CORES), ALL_AXES)
    expert = ("xh", "z", "y", "c")
    return jax.shard_map(
        per_device,
        mesh=fine,
        in_specs=(
            P(ALL_AXES, None),
            P(ALL_AXES, None),
            P(ALL_AXES, None),
            P(),
            P(expert, None, "dp"),
            P(expert, None, "dp"),
            P(expert, "dp", None),
        ),
        out_specs=P(ALL_AXES, None),
        check_vma=False,
    )
```

```python
import functools
import itertools

import jax
import jax.numpy as jnp
from jax import lax
from jax.experimental import pallas as pl
from jax.experimental.pallas import tpu as pltpu
from jax.sharding import Mesh, PartitionSpec as P

ALL_AXES = ("dp", "xh", "z", "y", "c")
RING = 4
CORES = 2
CAP = 4
TOP = 8
GROUP = 16
META = 128
MAIN = 2432
SIDE = 1152
BLOCK = 128
TAIL = MAIN + 2 * SIDE
SHIFTS = (0, 1, 3, 2)
MAIN_ROUTE = (("z", "y"), ("y", "x"), ("x", "z"))
SIDE_ROUTE = (("x", "x"), ("z", "z"), ("y", "y"))
TWIN_HOP = ("z", "x")
MIB = 1 << 20


def flat_index(x, z, y, c):
    return ((((x % 2) * 2 + x // 2) * RING + z) * RING + y) * CORES + c


def ring_perm(axes, shift):
    pairs = []
    for x, z, y, c in itertools.product(range(RING), range(RING), range(RING), range(CORES)):
        there = {"x": x, "z": z, "y": y}
        there[axes[c]] = (there[axes[c]] + shift) % RING
        pairs.append((flat_index(x, z, y, c), flat_index(there["x"], there["z"], there["y"], c)))
    return pairs


def moved_along(value, axes, shift):
    return lax.ppermute(value, ALL_AXES, ring_perm(axes, shift))


def other_core(value):
    return lax.ppermute(value, "c", [(0, 1), (1, 0)])


def gathered(value, axes):
    return [value] + [moved_along(value, axes, s) for s in SHIFTS[1:]]


def dealt(blocks, axes):
    return [blocks[0]] + [moved_along(b, axes, s) for b, s in zip(blocks[1:], SHIFTS[1:])]


def scattered(blocks, axes):
    return [blocks[0]] + [moved_along(b, axes, -s % RING) for b, s in zip(blocks[1:], SHIFTS[1:])]


def column_chunks(width):
    steps, start = [], 0
    while start < width:
        size = min(640, width - start)
        steps.append((start, size))
        start += size
    return steps


def iota(shape, dim):
    return lax.broadcasted_iota(jnp.int32, shape, dim)


def slots_of(meta, experts):
    turned = jnp.transpose(meta.astype(jnp.float32))
    owner = turned[:TOP]
    match = [owner == e.astype(jnp.float32) for e in experts]
    hits = [jnp.max(jnp.where(m, 1.0, 0.0), axis=0, keepdims=True) for m in match]
    stacked = jnp.concatenate(hits + [jnp.zeros((8 - RING, BLOCK), jnp.float32)], axis=0)
    row, col = iota((BLOCK, BLOCK), 0), iota((BLOCK, BLOCK), 1)
    before = jnp.where((row // GROUP == col // GROUP) & (row < col), 1.0, 0.0)
    rank = jnp.dot(stacked.astype(jnp.bfloat16), before.astype(jnp.bfloat16),
                   preferred_element_type=jnp.float32)
    base = (iota((1, BLOCK), 1) // GROUP * CAP).astype(jnp.float32)
    slot = iota((BLOCK // RING, BLOCK), 0).astype(jnp.float32)
    place = [slot == jnp.where(hits[r] > 0.5, base + rank[r:r + 1], -1.0) for r in range(RING)]
    return place, match, turned


def pack_kernel(first_expert, widths, info, *refs):
    pieces = len(widths)
    blocks = [refs[RING * i:RING * i + RING] for i in range(pieces)]
    outs = refs[RING * pieces:]
    experts = [info[first_expert + r] for r in range(RING)]
    rows = BLOCK // RING
    for b in range(RING):
        meta = blocks[0][b][:, widths[0]:widths[0] + META]
        place, _, _ = slots_of(meta, experts)
        spread = jnp.concatenate([jnp.where(p, 1.0, 0.0) for p in place], axis=0).astype(jnp.bfloat16)
        offset = 0
        for piece, width in zip(blocks, widths):
            for start, size in column_chunks(width):
                got = jnp.dot(spread, piece[b][:, start:start + size], preferred_element_type=jnp.float32)
                got = got.astype(jnp.bfloat16)
                for r in range(RING):
                    outs[r][rows * b:rows * (b + 1), offset + start:offset + start + size] = (
                        got[rows * r:rows * (r + 1)])
            offset += width


VMEM_SPEC = pl.BlockSpec(memory_space=pltpu.VMEM)
SMEM_SPEC = pl.BlockSpec(memory_space=pltpu.SMEM)
ANY_SPEC = pl.BlockSpec(memory_space=pl.ANY)


def pack(info, first_expert, *pieces):
    widths = [p[0].shape[1] - META for p in pieces]
    total = sum(widths)
    out = jax.ShapeDtypeStruct((BLOCK, total), jnp.bfloat16)
    return pl.pallas_call(
        functools.partial(pack_kernel, first_expert, widths),
        out_shape=[out] * RING,
        in_specs=[SMEM_SPEC] + [VMEM_SPEC] * (RING * len(pieces)),
        out_specs=[VMEM_SPEC] * RING,
        compiler_params=pltpu.CompilerParams(vmem_limit_bytes=24 * MIB),
        cost_estimate=pl.CostEstimate(
            flops=2 * RING * BLOCK * BLOCK * total, bytes_accessed=16 * BLOCK * total, transcendentals=0),
    )(info, *[b for p in pieces for b in p])


def combine_kernel(first_expert, width, joined, info, *refs):
    blocks, metas, rest = refs[:RING], refs[RING:2 * RING], refs[2 * RING:]
    if joined:
        outs = rest[0]
    else:
        add, outs = rest[0], rest[1:]
    experts = [info[first_expert + r] for r in range(RING)]
    rows = BLOCK // RING
    for b in range(RING):
        place, match, turned = slots_of(metas[b][...], experts)
        parts = []
        for offset in (TOP, 2 * TOP):
            mix = turned[offset:offset + TOP]
            picked = [jnp.sum(jnp.where(m, mix, 0.0), axis=0, keepdims=True) for m in match]
            weight = jnp.concatenate([jnp.where(p, w, 0.0) for p, w in zip(place, picked)], axis=0)
            parts.append(jnp.transpose(weight))
        mixer = jnp.concatenate(parts, axis=0).astype(jnp.bfloat16)
        for start, size in column_chunks(width):
            cols = slice(start, start + size)
            data = jnp.concatenate([blocks[r][rows * b:rows * (b + 1), cols] for r in range(RING)], axis=0)
            got = jnp.dot(mixer, data, preferred_element_type=jnp.float32)
            got = got[:BLOCK] + got[BLOCK:]
            if joined:
                outs[BLOCK * b:BLOCK * (b + 1), cols] = got.astype(jnp.bfloat16)
            else:
                got = got + add[BLOCK * b:BLOCK * (b + 1), cols].astype(jnp.float32)
                outs[b][:, cols] = got.astype(jnp.bfloat16)


def combine(info, first_expert, blocks, column, width, metas, meta_column, add=None):
    row_spec = pl.BlockSpec((BLOCK, width), lambda i: (0, column))
    meta_spec = pl.BlockSpec((BLOCK, META), lambda i: (0, meta_column))
    if add is None:
        out = jax.ShapeDtypeStruct((RING * BLOCK, width), jnp.bfloat16)
        extra, extra_specs, out_specs = [], [], VMEM_SPEC
    else:
        out = [jax.ShapeDtypeStruct((BLOCK, width), jnp.bfloat16)] * RING
        extra, extra_specs, out_specs = [add], [VMEM_SPEC], [VMEM_SPEC] * RING
    return pl.pallas_call(
        functools.partial(combine_kernel, first_expert, width, add is None),
        grid=(1,),
        out_shape=out,
        in_specs=[SMEM_SPEC] + [row_spec] * RING + [meta_spec] * RING + extra_specs,
        out_specs=out_specs,
        compiler_params=pltpu.CompilerParams(vmem_limit_bytes=24 * MIB),
        cost_estimate=pl.CostEstimate(
            flops=4 * RING * BLOCK * BLOCK * width, bytes_accessed=16 * BLOCK * width, transcendentals=0),
    )(info, *blocks, *metas, *extra)


def expert_kernel(info, *refs):
    inputs = [refs[4 * i:4 * i + 4] for i in range(3)]
    gate_hbm, up_hbm, down_hbm = refs[12:15]
    outputs = [refs[15 + 4 * i:19 + 4 * i] for i in range(3)]
    (x1, x2, xs, w_in, w_out, a1, a2, a_s, h1, h2, hs, o1, o2, o_s,
     x_sem, in_sem, down_sem, out_sem) = refs[27:]
    core = info[0]
    first = core == 0
    rows = RING * BLOCK
    at_main = pl.multiple_of(core * TAIL, BLOCK)
    at_twin = pl.multiple_of((1 - core) * TAIL, BLOCK)
    at_side = pl.multiple_of(MAIN + core * SIDE, BLOCK)
    at_far = pl.multiple_of(MAIN + (1 - core) * SIDE, BLOCK)
    chunks = []
    for part, width, base in ((0, MAIN, at_main), (1, MAIN, at_twin)):
        chunks += [(part, start, size, base + start) for start, size in column_chunks(width)]
    for half, base in ((0, at_side), (1, at_far)):
        chunks += [(2, half * SIDE + start, size, base + start) for start, size in column_chunks(SIDE)]
    starts = []
    total = 0
    for chunk in chunks:
        starts.append(total)
        total += chunk[2]

    x_parts, a_parts, h_parts, o_parts = (x1, x2, xs), (a1, a2, a_s), (h1, h2, hs), (o1, o2, o_s)
    x_copies = [
        [pltpu.make_async_copy(inputs[p][r], x_parts[p].at[pl.ds(r * BLOCK, BLOCK)], x_sem.at[4 * p + r])
         for r in range(RING)] for p in range(3)]
    in_copies, down_copies = [], []
    half = w_in.shape[1] // 2
    for i, ((part, off, size, col), at) in enumerate(zip(chunks, starts)):
        col = pl.multiple_of(col, BLOCK)
        in_copies.append((
            pltpu.make_async_copy(gate_hbm.at[pl.ds(col, size)], w_in.at[pl.ds(at, size), pl.ds(0, half)],
                                  in_sem.at[2 * i]),
            pltpu.make_async_copy(up_hbm.at[pl.ds(col, size)], w_in.at[pl.ds(at, size), pl.ds(half, half)],
                                  in_sem.at[2 * i + 1])))
        down_copies.append(pltpu.make_async_copy(
            down_hbm.at[:, pl.ds(col, size)], w_out.at[:, pl.ds(at, size)], down_sem.at[i]))
    seen = set()
    for (part, _, _, _), pair in zip(chunks, in_copies):
        if part not in seen:
            seen.add(part)
            for copy in x_copies[part]:
                copy.start()
        for copy in pair:
            copy.start()
    for copy in down_copies:
        copy.start()

    seen = set()
    for (part, off, size, _), at, pair in zip(chunks, starts, in_copies):
        fresh = part not in seen
        if fresh:
            seen.add(part)
            for copy in x_copies[part]:
                copy.wait()
        for copy in pair:
            copy.wait()
        got = jnp.dot(x_parts[part][:, off:off + size], w_in[at:at + size, :], preferred_element_type=jnp.float32)
        if fresh:
            a_parts[part][...] = got
        else:
            a_parts[part][...] += got

    def activate(i, carry):
        x, y, z = i // 16, i // 4 % 4, i % 4
        left, right = i, z * 16 + x * 4 + y
        i1 = pl.multiple_of(jnp.where(first, left, right) * 8, 8)
        i2 = pl.multiple_of(jnp.where(first, right, left) * 8, 8)
        i3 = pl.multiple_of((y * 16 + z * 4 + x) * 8, 8)
        both = a1[pl.ds(i1, 8)] + a2[pl.ds(i2, 8)] + a_s[pl.ds(i3, 8)]
        gate, up = both[:, :half], both[:, half:]
        value = gate / (1.0 + jnp.exp(-gate)) * up
        h1[pl.ds(i1, 8)] = value
        h2[pl.ds(i2, 8)] = value
        hs[pl.ds(i3, 8)] = value
        return carry

    lax.fori_loop(0, RING ** 3, activate, 0)
    hidden = [h[...].astype(jnp.bfloat16) for h in h_parts]
    out_copies = []
    for i, ((part, off, size, _), at, copy) in enumerate(zip(chunks, starts, down_copies)):
        copy.wait()
        got = jnp.dot(hidden[part], w_out[:, at:at + size], preferred_element_type=jnp.float32)
        o_parts[part][:, off:off + size] = got.astype(jnp.bfloat16)
        for r in range(RING):
            out = pltpu.make_async_copy(
                o_parts[part].at[pl.ds(r * BLOCK, BLOCK), pl.ds(off, size)],
                outputs[part][r].at[:, pl.ds(off, size)], out_sem.at[4 * i + r])
            out.start()
            out_copies.append(out)
    for out in out_copies:
        out.wait()


def expert(info, main, twin, side, gate_w, up_w, down_w):
    rows = RING * BLOCK
    width, hid = gate_w.shape
    n_chunks = 2 * len(column_chunks(MAIN)) + 2 * len(column_chunks(SIDE))
    block = lambda w: jax.ShapeDtypeStruct((BLOCK, w), jnp.bfloat16)
    bf, f32 = jnp.bfloat16, jnp.float32
    out = pl.pallas_call(
        expert_kernel,
        out_shape=[block(MAIN)] * 8 + [block(2 * SIDE)] * 4,
        in_specs=[SMEM_SPEC] + [ANY_SPEC] * 15,
        out_specs=[ANY_SPEC] * 12,
        scratch_shapes=[
            pltpu.VMEM((rows, MAIN), bf), pltpu.VMEM((rows, MAIN), bf), pltpu.VMEM((rows, 2 * SIDE), bf),
            pltpu.VMEM((width, 2 * hid), bf), pltpu.VMEM((hid, width), bf),
            pltpu.VMEM((rows, 2 * hid), f32), pltpu.VMEM((rows, 2 * hid), f32), pltpu.VMEM((rows, 2 * hid), f32),
            pltpu.VMEM((rows, hid), f32), pltpu.VMEM((rows, hid), f32), pltpu.VMEM((rows, hid), f32),
            pltpu.VMEM((rows, MAIN), bf), pltpu.VMEM((rows, MAIN), bf), pltpu.VMEM((rows, 2 * SIDE), bf),
            pltpu.SemaphoreType.DMA((12,)), pltpu.SemaphoreType.DMA((2 * n_chunks,)),
            pltpu.SemaphoreType.DMA((n_chunks,)), pltpu.SemaphoreType.DMA((4 * n_chunks,)),
        ],
        compiler_params=pltpu.CompilerParams(vmem_limit_bytes=56 * MIB),
        cost_estimate=pl.CostEstimate(
            flops=6 * rows * width * hid, bytes_accessed=2 * (3 * width * hid + 2 * rows * width),
            transcendentals=rows * hid),
    )(info, *main, *twin, *side, gate_w, up_w, down_w)
    return out[:4], out[4:8], out[8:]


def summed(blocks):
    return sum(b.astype(jnp.float32) for b in blocks).astype(jnp.bfloat16)


def split_rows(value):
    return list(value.reshape(RING, -1, value.shape[-1]))


def per_device(tokens, picks, mix_weights, pairs, gate_weight, up_weight, down_weight):
    tok_rows, width = tokens.shape
    c = lax.axis_index("c")
    x = lax.axis_index("xh") * 2 + lax.axis_index("dp")
    z = lax.axis_index("z")
    y = lax.axis_index("y")
    first = c == 0

    shifts = jnp.array(SHIFTS, jnp.int32)
    place = lambda x, z, y: ((x // 2 * RING + z) * RING + y) * CORES + c + 0 * shifts
    along_x = place((x + shifts) % RING, z, y)
    along_z = place(x, (z + shifts) % RING, y)
    along_y = place(x, z, (y + shifts) % RING)
    info = jnp.concatenate([
        jnp.stack([c, c, c, c]), jnp.where(first, along_x, along_z), jnp.where(first, along_z, along_x), along_y
    ]).astype(jnp.int32)
    at_main, at_twin, at_side = 4, 8, 12

    moved = jnp.any(picks[:, :, None] == pairs.reshape(-1), axis=-1)
    owner = jnp.where(moved, picks ^ 32, picks)
    mix_hi = lax.reduce_precision(mix_weights, 8, 7)
    meta = jnp.concatenate([owner.astype(jnp.float32), mix_hi, mix_weights - mix_hi], axis=1)
    meta = jnp.pad(meta, ((0, 0), (0, META - 3 * TOP))).astype(jnp.bfloat16)

    left = jnp.concatenate([tokens[:, :MAIN], meta, tokens[:, MAIN:MAIN + SIDE], meta], axis=1)
    right = jnp.concatenate([tokens[:, TAIL:], meta, tokens[:, MAIN + SIDE:TAIL], meta], axis=1)
    mine = jnp.where(first, left, right)
    theirs = other_core(jnp.where(first, right, left))
    both = jnp.where(first, jnp.concatenate([mine, theirs]), jnp.concatenate([theirs, mine]))
    main, side = both[:, :MAIN + META], both[:, MAIN + META:]
    main = jnp.concatenate(gathered(main, MAIN_ROUTE[0]), axis=0)
    side = jnp.concatenate(gathered(side, SIDE_ROUTE[0]), axis=0)
    main = gathered(main, MAIN_ROUTE[1])
    side = gathered(side, SIDE_ROUTE[1])
    twin = [other_core(b) for b in main]
    far = [other_core(b) for b in side]

    main_in = dealt(pack(info, at_main, main), MAIN_ROUTE[2])
    twin_in = dealt(pack(info, at_twin, twin), TWIN_HOP)
    side_in = dealt(pack(info, at_side, side, far), SIDE_ROUTE[2])

    main_out, twin_out, side_out = expert(
        info, main_in, twin_in, side_in, gate_weight[0], up_weight[0], down_weight[0])

    twin_back = scattered(twin_out, TWIN_HOP)
    side_back = scattered(side_out, SIDE_ROUTE[2])
    main_back = scattered(main_out, MAIN_ROUTE[2])
    main_meta, side_meta = MAIN // META, SIDE // META
    main_add = other_core(combine(info, at_twin, twin_back, 0, MAIN, twin, main_meta))
    side_add = other_core(combine(info, at_side, side_back, 1, SIDE, side, side_meta))
    main = combine(info, at_main, main_back, 0, MAIN, main, main_meta, main_add)
    side = combine(info, at_side, side_back, 0, SIDE, side, side_meta, side_add)
    main = summed(scattered(main, MAIN_ROUTE[1]))
    side = summed(scattered(side, SIDE_ROUTE[1]))
    main = summed(scattered(split_rows(main), MAIN_ROUTE[0]))
    side = summed(scattered(split_rows(side), SIDE_ROUTE[0]))
    done = jnp.concatenate([main, side], axis=1)
    own = jnp.where(first, done[:tok_rows], done[tok_rows:])
    rest = other_core(jnp.where(first, done[tok_rows:], done[:tok_rows]))
    lower = jnp.where(first, own, rest)
    upper = jnp.where(first, rest, own)
    return jnp.concatenate([lower, upper[:, MAIN:], upper[:, :MAIN]], axis=1)


def solution(mesh):
    fine = Mesh(mesh.devices.reshape(2, 2, RING, RING, CORES), ALL_AXES)
    experts = ("xh", "z", "y", "c")
    return jax.shard_map(
        per_device,
        mesh=fine,
        in_specs=(
            P(ALL_AXES, None),
            P(ALL_AXES, None),
            P(ALL_AXES, None),
            P(),
            P(experts, None, "dp"),
            P(experts, None, "dp"),
            P(experts, "dp", None),
        ),
        out_specs=P(ALL_AXES, None),
        check_vma=False,
    )
```

```python
import functools
import itertools

import jax
import jax.numpy as jnp
from jax import lax
from jax.experimental import pallas as pl
from jax.experimental.pallas import tpu as pltpu
from jax.sharding import Mesh, PartitionSpec as P

ALL_AXES = ("dp", "xh", "z", "y", "c")
RING = 4
CORES = 2
CAP = 4
TOP = 8
GROUP = 16
META = 128
MAIN = 2560
SIDE = 1024
BLOCK = 128
TAIL = MAIN + 2 * SIDE
SHIFTS = (0, 1, 3, 2)
MAIN_ROUTE = (("z", "y"), ("y", "x"), ("x", "z"))
SIDE_ROUTE = (("x", "x"), ("z", "z"), ("y", "y"))
SMALL_VMEM = 24 << 20
LARGE_VMEM = 56 << 20


def flat_index(x, z, y, c):
    return ((((x % 2) * 2 + x // 2) * RING + z) * RING + y) * CORES + c


def ring_perm(axes, shift, cross=False):
    pairs = []
    for x, z, y, c in itertools.product(range(RING), range(RING), range(RING), range(CORES)):
        there = {"x": x, "z": z, "y": y}
        there[axes[c]] = (there[axes[c]] + shift) % RING
        target = flat_index(there["x"], there["z"], there["y"], 1 - c if cross else c)
        pairs.append((flat_index(x, z, y, c), target))
    return pairs


def together(*values):
    return lax.optimization_barrier(values)


def back_perm(axes, shift, cross=False):
    return [(target, source) for source, target in ring_perm(axes, shift, cross)]


def gathered(value, axes):
    return [value] + [lax.ppermute(value, ALL_AXES, ring_perm(axes, s)) for s in SHIFTS[1:]]


def scattered(blocks, axes):
    return [blocks[0]] + [lax.ppermute(b, ALL_AXES, back_perm(axes, s)) for b, s in zip(blocks[1:], SHIFTS[1:])]


def other_core(value):
    return lax.ppermute(value, "c", [(0, 1), (1, 0)])


def hop(blocks, axes, perm, numbers, cross=False):
    return [other_core(blocks[r]) if r == 0 else lax.ppermute(blocks[r], ALL_AXES, perm(axes, SHIFTS[r], cross))
            for r in numbers]


def column_chunks(width):
    steps, start = [], 0
    while start < width:
        size = min(1280, width - start)
        steps.append((start, size))
        start += size
    return steps


def iota(shape, dim):
    return lax.broadcasted_iota(jnp.int32, shape, dim)


def slots_of(meta, experts):
    turned = jnp.transpose(meta.astype(jnp.float32))
    owner = turned[:TOP]
    match = [owner == e.astype(jnp.float32) for e in experts]
    hits = [jnp.max(jnp.where(m, 1.0, 0.0), axis=0, keepdims=True) for m in match]
    stacked = jnp.concatenate(hits, axis=0)
    row, col = iota((BLOCK, BLOCK), 0), iota((BLOCK, BLOCK), 1)
    before = jnp.where((row // GROUP == col // GROUP) & (row < col), 1.0, 0.0)
    rank = jnp.dot(stacked.astype(jnp.bfloat16), before.astype(jnp.bfloat16),
                   preferred_element_type=jnp.float32)
    base = (iota((1, BLOCK), 1) // GROUP * CAP).astype(jnp.float32)
    slot = iota((BLOCK // RING, BLOCK), 0).astype(jnp.float32)
    place = [slot == jnp.where(h > 0.5, base + rank[e:e + 1], -1.0) for e, h in enumerate(hits)]
    return place, match, turned


def experts_at(info, first_expert, cores):
    own = [info[first_expert + r] for r in range(RING)]
    return own + [e ^ 1 for e in own] if cores == CORES else own


def pack_kernel(first_expert, width, pieces, info, *refs):
    blocks, outs = [refs[RING * i:RING * i + RING] for i in range(pieces)], refs[RING * pieces:]
    experts = experts_at(info, first_expert, len(outs) // RING)
    rows = BLOCK // RING
    for b in range(RING):
        place, _, _ = slots_of(blocks[0][b][:, width:width + META], experts)
        spread = jnp.concatenate([jnp.where(p, 1.0, 0.0) for p in place], axis=0).astype(jnp.bfloat16)
        for piece in range(pieces):
            for start, size in column_chunks(width):
                got = jnp.dot(spread, blocks[piece][b][:, start:start + size], preferred_element_type=jnp.float32)
                got = got.astype(jnp.bfloat16)
                at = piece * width + start
                for e, out in enumerate(outs):
                    out[rows * b:rows * (b + 1), at:at + size] = got[rows * e:rows * (e + 1)]


VMEM_SPEC = pl.BlockSpec(memory_space=pltpu.VMEM)
SMEM_SPEC = pl.BlockSpec(memory_space=pltpu.SMEM)
HBM_SPEC = pl.BlockSpec(memory_space=pltpu.HBM)


def pack(info, first_expert, cores, *pieces):
    width = pieces[0][0].shape[1] - META
    total = width * len(pieces)
    out = pl.pallas_call(
        functools.partial(pack_kernel, first_expert, width, len(pieces)),
        out_shape=[jax.ShapeDtypeStruct((BLOCK, total), jnp.bfloat16)] * (cores * RING),
        in_specs=[SMEM_SPEC] + [VMEM_SPEC] * (RING * len(pieces)),
        out_specs=[VMEM_SPEC] * (cores * RING),
        compiler_params=pltpu.CompilerParams(vmem_limit_bytes=SMALL_VMEM),
        cost_estimate=pl.CostEstimate(
            flops=2 * cores * RING * BLOCK * BLOCK * total, bytes_accessed=16 * BLOCK * total, transcendentals=0),
    )(info, *[b for p in pieces for b in p])
    return list(out[:RING]), list(out[RING:])


def combine_kernel(first_expert, width, count, mode, info, *refs):
    blocks, metas, rest = refs[:count], refs[count:count + RING], refs[count + RING:]
    experts = experts_at(info, first_expert, count // RING)
    rows = BLOCK // RING
    for b in range(RING):
        place, match, turned = slots_of(metas[b][...], experts)
        parts = []
        for offset in (TOP, 2 * TOP):
            mix = turned[offset:offset + TOP]
            picked = [jnp.sum(jnp.where(m, mix, 0.0), axis=0, keepdims=True) for m in match]
            weight = jnp.concatenate([jnp.where(p, w, 0.0) for p, w in zip(place, picked)], axis=0)
            parts.append(jnp.transpose(weight))
        mixer = jnp.concatenate(parts, axis=0).astype(jnp.bfloat16)
        for start, size in column_chunks(width):
            cols = slice(start, start + size)
            data = jnp.concatenate([block[rows * b:rows * (b + 1), cols] for block in blocks], axis=0)
            got = jnp.dot(mixer, data, preferred_element_type=jnp.float32)
            got = got[:BLOCK] + got[BLOCK:]
            if mode == "add":
                got = got + rest[0][BLOCK * b:BLOCK * (b + 1), cols].astype(jnp.float32)
            if mode == "joined":
                rest[0][BLOCK * b:BLOCK * (b + 1), cols] = got.astype(jnp.bfloat16)
            else:
                rest[-RING + b][:, cols] = got.astype(jnp.bfloat16)


def combine(info, first_expert, blocks, metas, width, column=0, mode="blocks", add=None):
    row_spec = pl.BlockSpec((BLOCK, width), lambda i: (0, column))
    meta_spec = pl.BlockSpec((BLOCK, META), lambda i: (0, width // META))
    extra = [] if add is None else [add]
    if mode == "joined":
        out, out_specs = jax.ShapeDtypeStruct((RING * BLOCK, width), jnp.bfloat16), VMEM_SPEC
    else:
        out, out_specs = [jax.ShapeDtypeStruct((BLOCK, width), jnp.bfloat16)] * RING, [VMEM_SPEC] * RING
    return pl.pallas_call(
        functools.partial(combine_kernel, first_expert, width, len(blocks), mode),
        grid=(1,),
        out_shape=out,
        in_specs=[SMEM_SPEC] + [row_spec] * len(blocks) + [meta_spec] * RING + [VMEM_SPEC] * len(extra),
        out_specs=out_specs,
        compiler_params=pltpu.CompilerParams(vmem_limit_bytes=SMALL_VMEM),
        cost_estimate=pl.CostEstimate(
            flops=4 * len(blocks) * BLOCK * BLOCK * width, bytes_accessed=24 * BLOCK * width, transcendentals=0),
    )(info, *blocks, *metas, *extra)


def weight_copies(chunks, gate_hbm, up_hbm, w_in, in_sem):
    half = w_in.shape[1] // 2
    copies, at = [], 0
    for i, (col, size) in enumerate(chunks):
        col = pl.multiple_of(col, BLOCK)
        copies.append((
            pltpu.make_async_copy(gate_hbm.at[pl.ds(col, size)], w_in.at[pl.ds(at, size), pl.ds(0, half)],
                                  in_sem.at[2 * i]),
            pltpu.make_async_copy(up_hbm.at[pl.ds(col, size)], w_in.at[pl.ds(at, size), pl.ds(half, half)],
                                  in_sem.at[2 * i + 1])))
        at += size
    return copies


def block_copies(blocks, target, sems, first):
    return [pltpu.make_async_copy(blocks[r], target.at[pl.ds(r * BLOCK, BLOCK)], sems.at[first + r])
            for r in range(RING)]


def start_all(copies):
    for copy in copies:
        copy.start()


def wait_all(copies):
    for copy in copies:
        copy.wait()


def project_kernel(info, *refs):
    blocks, (gate_hbm, up_hbm, total, x, w_in, x_sem, in_sem) = refs[:RING], refs[RING:]
    base = info[0] * TAIL
    steps = column_chunks(MAIN)
    x_copies = block_copies(blocks, x, x_sem, 0)
    in_copies = weight_copies([(base + start, size) for start, size in steps], gate_hbm, up_hbm, w_in, in_sem)
    start_all(x_copies)
    for pair in in_copies:
        start_all(pair)
    wait_all(x_copies)
    for (start, size), pair in zip(steps, in_copies):
        wait_all(pair)
        cols = slice(start, start + size)
        got = jnp.dot(x[:, cols], w_in[cols, :], preferred_element_type=jnp.float32)
        if start == 0:
            total[...] = got
        else:
            total[...] += got


def project(info, blocks, gate_w, up_w):
    rows, hid = RING * BLOCK, gate_w.shape[1]
    return pl.pallas_call(
        project_kernel,
        out_shape=jax.ShapeDtypeStruct((rows, 2 * hid), jnp.float32),
        in_specs=[SMEM_SPEC] + [HBM_SPEC] * 6,
        out_specs=VMEM_SPEC,
        scratch_shapes=[
            pltpu.VMEM((rows, MAIN), jnp.bfloat16), pltpu.VMEM((MAIN, 2 * hid), jnp.bfloat16),
            pltpu.SemaphoreType.DMA((RING,)), pltpu.SemaphoreType.DMA((2 * len(column_chunks(MAIN)),)),
        ],
        compiler_params=pltpu.CompilerParams(vmem_limit_bytes=LARGE_VMEM),
        cost_estimate=pl.CostEstimate(
            flops=4 * rows * MAIN * hid, bytes_accessed=2 * (2 * MAIN * hid + rows * MAIN), transcendentals=0),
    )(info, *blocks, gate_w, up_w)


def expert_kernel(info, *refs):
    near, far, side = refs[0], refs[1:1 + RING], refs[1 + RING:1 + 2 * RING]
    gate_hbm, up_hbm, down_hbm = refs[9:12]
    main_outs, side_outs, hidden_far = refs[12:16], refs[16:20], refs[20]
    (x2, xs, w_in, w_out, a1, a2, a_s, h1, h2, hs, o1, o_s,
     x_sem, in_sem, down_sem, out_sem) = refs[21:]
    core = info[0]
    first = core == 0
    half = w_in.shape[1] // 2
    at_main, at_far = core * TAIL, (1 - core) * TAIL
    at_side = (MAIN + core * SIDE, MAIN + (1 - core) * SIDE)
    main_steps, side_steps = column_chunks(MAIN), column_chunks(SIDE)

    steps = [(xs, a_s, h * SIDE + start, size, at_side[h] + start) for h in range(2) for start, size in side_steps]
    steps += [(x2, a2, start, size, at_far + start) for start, size in main_steps]
    side_copies, far_copies = block_copies(side, xs, x_sem, 0), block_copies(far, x2, x_sem, RING)
    near_copy = pltpu.make_async_copy(near, a1, x_sem.at[2 * RING])
    in_copies = weight_copies([step[3:][::-1] for step in steps], gate_hbm, up_hbm, w_in, in_sem)
    outs = [(0, o1, main_outs, start, size, at_main + start) for start, size in main_steps]
    outs += [(1, o_s, side_outs, h * SIDE + start, size, at_side[h] + start)
             for h in range(2) for start, size in side_steps]
    down_copies, at = [], 0
    for i, (_, _, _, _, size, col) in enumerate(outs):
        down_copies.append(pltpu.make_async_copy(
            down_hbm.at[:, pl.ds(pl.multiple_of(col, BLOCK), size)], w_out.at[:, pl.ds(at, size)], down_sem.at[i]))
        at += size
    start_all(side_copies)
    start_all(in_copies[0])
    start_all(far_copies)
    for pair in in_copies[1:]:
        start_all(pair)
    near_copy.start()
    start_all(down_copies)

    at = 0
    for (x, total, off, size, _), pair in zip(steps, in_copies):
        if off == 0:
            wait_all(side_copies if x is xs else far_copies)
        wait_all(pair)
        got = jnp.dot(x[:, off:off + size], w_in[at:at + size, :], preferred_element_type=jnp.float32)
        if off == 0:
            total[...] = got
        else:
            total[...] += got
        at += size
    near_copy.wait()

    def activate(i, carry):
        x, y, z = i // 16, i // 4 % 4, i % 4
        left, right = i, z * 16 + x * 4 + y
        i1 = pl.multiple_of(jnp.where(first, left, right) * 8, 8)
        i2 = pl.multiple_of(jnp.where(first, right, left) * 8, 8)
        i3 = pl.multiple_of((y * 16 + z * 4 + x) * 8, 8)
        both = a1[pl.ds(i1, 8)] + a2[pl.ds(i2, 8)] + a_s[pl.ds(i3, 8)]
        gate, up = both[:, :half], both[:, half:]
        value = gate / (1.0 + jnp.exp(-gate)) * up
        h1[pl.ds(i1, 8)] = value
        h2[pl.ds(i2, 8)] = value
        hs[pl.ds(i3, 8)] = value
        return carry

    lax.fori_loop(0, RING ** 3, activate, 0, unroll=4)
    hidden_far[...] = h2[...].astype(jnp.bfloat16)
    hidden = (h1[...].astype(jnp.bfloat16), hs[...].astype(jnp.bfloat16))
    out_copies, at = [], 0
    for i, ((part, rows, targets, off, size, _), copy) in enumerate(zip(outs, down_copies)):
        copy.wait()
        got = jnp.dot(hidden[part], w_out[:, at:at + size], preferred_element_type=jnp.float32)
        rows[:, off:off + size] = got.astype(jnp.bfloat16)
        for r in range(RING):
            out_copies.append(pltpu.make_async_copy(
                rows.at[pl.ds(r * BLOCK, BLOCK), pl.ds(off, size)],
                targets[r].at[:, pl.ds(off, size)], out_sem.at[RING * i + r]))
            out_copies[-1].start()
        at += size
    wait_all(out_copies)


def expert(info, near, far, side, gate_w, up_w, down_w):
    rows, (width, hid) = RING * BLOCK, gate_w.shape
    n_main, n_side = len(column_chunks(MAIN)), len(column_chunks(SIDE))
    part = MAIN + 2 * SIDE
    block = lambda w: jax.ShapeDtypeStruct((BLOCK, w), jnp.bfloat16)
    bf, f32 = jnp.bfloat16, jnp.float32
    out = pl.pallas_call(
        expert_kernel,
        out_shape=[block(MAIN)] * RING + [block(2 * SIDE)] * RING + [jax.ShapeDtypeStruct((rows, hid), bf)],
        in_specs=[SMEM_SPEC] + [HBM_SPEC] * 12,
        out_specs=[HBM_SPEC] * 8 + [VMEM_SPEC],
        scratch_shapes=[
            pltpu.VMEM((rows, MAIN), bf), pltpu.VMEM((rows, 2 * SIDE), bf),
            pltpu.VMEM((part, 2 * hid), bf), pltpu.VMEM((hid, part), bf),
            pltpu.VMEM((rows, 2 * hid), f32), pltpu.VMEM((rows, 2 * hid), f32), pltpu.VMEM((rows, 2 * hid), f32),
            pltpu.VMEM((rows, hid), f32), pltpu.VMEM((rows, hid), f32), pltpu.VMEM((rows, hid), f32),
            pltpu.VMEM((rows, MAIN), bf), pltpu.VMEM((rows, 2 * SIDE), bf),
            pltpu.SemaphoreType.DMA((2 * RING + 1,)), pltpu.SemaphoreType.DMA((2 * (n_main + 2 * n_side),)),
            pltpu.SemaphoreType.DMA((n_main + 2 * n_side,)),
            pltpu.SemaphoreType.DMA((RING * (n_main + 2 * n_side),)),
        ],
        compiler_params=pltpu.CompilerParams(vmem_limit_bytes=LARGE_VMEM),
        cost_estimate=pl.CostEstimate(
            flops=6 * rows * part * hid, bytes_accessed=2 * (3 * part * hid + 2 * rows * part),
            transcendentals=rows * hid),
    )(info, near, *far, *side, gate_w, up_w, down_w)
    return list(out[:RING]), list(out[RING:2 * RING]), out[2 * RING]


def spread_kernel(info, hidden, down_hbm, *refs):
    outs, (w_out, down_sem) = refs[:RING], refs[RING:]
    base = (1 - info[0]) * TAIL
    steps = column_chunks(MAIN)
    copies = [pltpu.make_async_copy(
        down_hbm.at[:, pl.ds(pl.multiple_of(base + start, BLOCK), size)], w_out.at[:, pl.ds(start, size)],
        down_sem.at[i]) for i, (start, size) in enumerate(steps)]
    start_all(copies)
    for (start, size), copy in zip(steps, copies):
        copy.wait()
        cols = slice(start, start + size)
        got = jnp.dot(hidden[...], w_out[:, cols], preferred_element_type=jnp.float32).astype(jnp.bfloat16)
        for r in range(RING):
            outs[r][:, cols] = got[BLOCK * r:BLOCK * (r + 1)]


def spread(info, hidden, down_w):
    rows, hid = hidden.shape
    out = pl.pallas_call(
        spread_kernel,
        out_shape=[jax.ShapeDtypeStruct((BLOCK, MAIN), jnp.bfloat16)] * RING,
        in_specs=[SMEM_SPEC, VMEM_SPEC, HBM_SPEC],
        out_specs=[VMEM_SPEC] * RING,
        scratch_shapes=[
            pltpu.VMEM((hid, MAIN), jnp.bfloat16), pltpu.SemaphoreType.DMA((len(column_chunks(MAIN)),))],
        compiler_params=pltpu.CompilerParams(vmem_limit_bytes=LARGE_VMEM),
        cost_estimate=pl.CostEstimate(
            flops=2 * rows * MAIN * hid, bytes_accessed=2 * MAIN * (hid + rows), transcendentals=0),
    )(info, hidden, down_w)
    return list(out)


def summed(blocks):
    return sum(b.astype(jnp.float32) for b in blocks).astype(jnp.bfloat16)


def split_rows(value):
    return list(value.reshape(RING, -1, value.shape[-1]))


def per_device(tokens, picks, mix_weights, pairs, gate_weight, up_weight, down_weight):
    tok_rows, width = tokens.shape
    c = lax.axis_index("c")
    x = lax.axis_index("xh") * 2 + lax.axis_index("dp")
    z = lax.axis_index("z")
    y = lax.axis_index("y")
    first = c == 0

    shifts = jnp.array(SHIFTS, jnp.int32)
    place = lambda x, z, y: ((x // 2 * RING + z) * RING + y) * CORES + c + 0 * shifts
    along_x = place((x + shifts) % RING, z, y)
    along_z = place(x, (z + shifts) % RING, y)
    along_y = place(x, z, (y + shifts) % RING)
    info = jnp.concatenate([jnp.stack([c, c, c, c]), jnp.where(first, along_x, along_z), along_y]).astype(jnp.int32)
    at_main, at_side = 4, 8

    moved = jnp.any(picks[:, :, None] == pairs.reshape(-1), axis=-1)
    owner = jnp.where(moved, picks ^ 32, picks)
    mix_hi = lax.reduce_precision(mix_weights, 8, 7)
    meta = jnp.concatenate([owner.astype(jnp.float32), mix_hi, mix_weights - mix_hi], axis=1)
    meta = jnp.pad(meta, ((0, 0), (0, META - 3 * TOP))).astype(jnp.bfloat16)

    left = jnp.concatenate([tokens[:, :MAIN], meta, tokens[:, MAIN:MAIN + SIDE], meta], axis=1)
    right = jnp.concatenate([tokens[:, TAIL:], meta, tokens[:, MAIN + SIDE:TAIL], meta], axis=1)
    mine = jnp.where(first, left, right)
    theirs = other_core(jnp.where(first, right, left))
    both = jnp.where(first, jnp.concatenate([mine, theirs]), jnp.concatenate([theirs, mine]))
    main, side = both[:, :MAIN + META], both[:, MAIN + META:]
    main, side = together(gathered(main, MAIN_ROUTE[0]), gathered(side, SIDE_ROUTE[0]))
    main, side = together(jnp.concatenate(main, axis=0), jnp.concatenate(side, axis=0))
    main, side = together(gathered(main, MAIN_ROUTE[1]), gathered(side, SIDE_ROUTE[1]))

    main_hop, side_hop = MAIN_ROUTE[2], SIDE_ROUTE[2]
    side_far = [other_core(b) for b in side]
    main_own, main_far = pack(info, at_main, CORES, main)
    main_own, side_far = together(main_own, side_far)
    own, here = together(hop(main_own, main_hop, ring_perm, (1, 2, 3)), hop(main_far, main_hop, ring_perm, (0,)))
    side_own, _ = pack(info, at_side, 1, side, side_far)
    across = hop(side_own, side_hop, ring_perm, (3,))
    main_far, side_own, own = together(main_far, side_own, own)
    far = hop(main_far, main_hop, ring_perm, (1, 2, 3), cross=True)
    beside = hop(side_own, side_hop, ring_perm, (1, 2))
    gate_w, up_w, down_w = gate_weight[0], up_weight[0], down_weight[0]
    near = project(info, main_own[:1] + own, gate_w, up_w)
    far, beside, across = together(far, beside, across)
    main_own, side_own, hidden = expert(
        info, near, here + far, side_own[:1] + beside + across, gate_w, up_w, down_w)
    main_far = spread(info, hidden, down_w)
    own, beside = together(
        hop(main_own, main_hop, back_perm, (1, 2, 3)), hop(side_own, side_hop, back_perm, (1, 2)))
    main_far, side_own, own = together(main_far, side_own, own)
    far, across = together(
        hop(main_far, main_hop, back_perm, (1, 2, 3, 0), cross=True), hop(side_own, side_hop, back_perm, (3,)))
    main_own = main_own[:1] + own
    main_far = far[3:] + far[:3]
    side_own = side_own[:1] + beside + across
    side_add = other_core(combine(info, at_side, side_own, side, SIDE, 1, "joined"))
    main = combine(info, at_main, main_own + main_far, main, MAIN)
    side = combine(info, at_side, side_own, side, SIDE, 0, "add", side_add)
    main, side = together(scattered(main, MAIN_ROUTE[1]), scattered(side, SIDE_ROUTE[1]))
    main, side = together(summed(main), summed(side))
    main, side = together(
        scattered(split_rows(main), MAIN_ROUTE[0]), scattered(split_rows(side), SIDE_ROUTE[0]))
    main, side = summed(main), summed(side)
    done = jnp.concatenate([main, side], axis=1)
    own = jnp.where(first, done[:tok_rows], done[tok_rows:])
    rest = other_core(jnp.where(first, done[tok_rows:], done[:tok_rows]))
    lower = jnp.where(first, own, rest)
    upper = jnp.where(first, rest, own)
    return jnp.concatenate([lower, upper[:, MAIN:], upper[:, :MAIN]], axis=1)


def solution(mesh):
    fine = Mesh(mesh.devices.reshape(2, 2, RING, RING, CORES), ALL_AXES)
    experts = ("xh", "z", "y", "c")
    return jax.shard_map(
        per_device,
        mesh=fine,
        in_specs=(
            P(ALL_AXES, None),
            P(ALL_AXES, None),
            P(ALL_AXES, None),
            P(),
            P(experts, None, "dp"),
            P(experts, None, "dp"),
            P(experts, "dp", None),
        ),
        out_specs=P(ALL_AXES, None),
        check_vma=False,
    )
```

```python
import functools
import itertools

import jax
import jax.numpy as jnp
from jax import lax
from jax.experimental import pallas as pl
from jax.experimental.pallas import tpu as pltpu
from jax.sharding import Mesh, PartitionSpec as P

ALL_AXES = ("dp", "xh", "z", "y", "c")
RING = 4
CORES = 2
CAP = 4
TOP = 8
GROUP = 16
META = 128
HALF = 3584
BLOCK = 128
SHIFTS = (0, 1, 3, 2)
ROUTE = (("z", "y"), ("y", "x"), ("x", "z"))
SMALL_VMEM = 24 << 20
LARGE_VMEM = 56 << 20


def flat_index(x, z, y, c):
    return ((((x % 2) * 2 + x // 2) * RING + z) * RING + y) * CORES + c


def ring_perm(axes, shift, cross=False):
    pairs = []
    for x, z, y, c in itertools.product(range(RING), range(RING), range(RING), range(CORES)):
        there = {"x": x, "z": z, "y": y}
        there[axes[c]] = (there[axes[c]] + shift) % RING
        target = flat_index(there["x"], there["z"], there["y"], 1 - c if cross else c)
        pairs.append((flat_index(x, z, y, c), target))
    return pairs


def together(*values):
    return lax.optimization_barrier(values)


def back_perm(axes, shift, cross=False):
    return [(target, source) for source, target in ring_perm(axes, shift, cross)]


def gathered(value, axes):
    return [value] + [lax.ppermute(value, ALL_AXES, ring_perm(axes, s)) for s in SHIFTS[1:]]


def scattered(blocks, axes):
    return [blocks[0]] + [lax.ppermute(b, ALL_AXES, back_perm(axes, s)) for b, s in zip(blocks[1:], SHIFTS[1:])]


def other_core(value):
    return lax.ppermute(value, "c", [(0, 1), (1, 0)])


def hop(blocks, axes, perm, numbers, cross=False):
    return [other_core(blocks[r]) if r == 0 else lax.ppermute(blocks[r], ALL_AXES, perm(axes, SHIFTS[r], cross))
            for r in numbers]


def column_chunks(width):
    steps, start = [], 0
    while start < width:
        size = min(1792, width - start)
        steps.append((start, size))
        start += size
    return steps


def iota(shape, dim):
    return lax.broadcasted_iota(jnp.int32, shape, dim)


def slots_of(meta, experts):
    turned = jnp.transpose(meta.astype(jnp.float32))
    owner = turned[:TOP]
    match = [owner == e.astype(jnp.float32) for e in experts]
    hits = [jnp.max(jnp.where(m, 1.0, 0.0), axis=0, keepdims=True) for m in match]
    stacked = jnp.concatenate(hits * (8 // len(hits)), axis=0)
    row, col = iota((BLOCK, BLOCK), 0), iota((BLOCK, BLOCK), 1)
    before = jnp.where((row // GROUP == col // GROUP) & (row < col), 1.0, 0.0)
    rank = jnp.dot(stacked.astype(jnp.bfloat16), before.astype(jnp.bfloat16),
                   preferred_element_type=jnp.float32)
    base = (iota((1, BLOCK), 1) // GROUP * CAP).astype(jnp.float32)
    slot = iota((BLOCK // RING, BLOCK), 0).astype(jnp.float32)
    place = [slot == jnp.where(h > 0.5, base + rank[e:e + 1], -1.0) for e, h in enumerate(hits)]
    return place, match, turned


def experts_at(info):
    own = [info[4 + r] for r in range(RING)]
    return own + [e ^ 1 for e in own]


def pack_kernel(cross, info, *refs):
    blocks, outs = refs[:RING], refs[RING:]
    experts = experts_at(info)[RING * cross:RING * cross + RING]
    rows = BLOCK // RING
    for b in range(RING):
        place, _, _ = slots_of(blocks[b][:, HALF:HALF + META], experts)
        spread = jnp.concatenate([jnp.where(p, 1.0, 0.0) for p in place], axis=0).astype(jnp.bfloat16)
        for start, size in column_chunks(HALF):
            cols = slice(start, start + size)
            got = jnp.dot(spread, blocks[b][:, cols], preferred_element_type=jnp.float32).astype(jnp.bfloat16)
            for e, out in enumerate(outs):
                out[rows * b:rows * (b + 1), cols] = got[rows * e:rows * (e + 1)]


VMEM_SPEC = pl.BlockSpec(memory_space=pltpu.VMEM)
SMEM_SPEC = pl.BlockSpec(memory_space=pltpu.SMEM)
HBM_SPEC = pl.BlockSpec(memory_space=pltpu.HBM)


def pack(info, blocks, cross):
    return list(pl.pallas_call(
        functools.partial(pack_kernel, cross),
        out_shape=[jax.ShapeDtypeStruct((BLOCK, HALF), jnp.bfloat16)] * RING,
        in_specs=[SMEM_SPEC] + [VMEM_SPEC] * RING,
        out_specs=[VMEM_SPEC] * RING,
        compiler_params=pltpu.CompilerParams(vmem_limit_bytes=SMALL_VMEM),
        cost_estimate=pl.CostEstimate(
            flops=2 * RING * BLOCK * BLOCK * HALF, bytes_accessed=16 * BLOCK * HALF, transcendentals=0),
    )(info, *blocks))


def combine_kernel(info, *refs):
    blocks, metas, outs = refs[:2 * RING], refs[2 * RING:3 * RING], refs[3 * RING:]
    experts = experts_at(info)
    rows = BLOCK // RING
    for b in range(RING):
        place, match, turned = slots_of(metas[b][...], experts)
        parts = []
        for offset in (TOP, 2 * TOP):
            mix = turned[offset:offset + TOP]
            picked = [jnp.sum(jnp.where(m, mix, 0.0), axis=0, keepdims=True) for m in match]
            weight = jnp.concatenate([jnp.where(p, w, 0.0) for p, w in zip(place, picked)], axis=0)
            parts.append(jnp.transpose(weight))
        mixer = jnp.concatenate(parts, axis=0).astype(jnp.bfloat16)
        for start, size in column_chunks(HALF):
            cols = slice(start, start + size)
            data = jnp.concatenate([block[rows * b:rows * (b + 1), cols] for block in blocks], axis=0)
            got = jnp.dot(mixer, data, preferred_element_type=jnp.float32)
            outs[b][:, cols] = (got[:BLOCK] + got[BLOCK:]).astype(jnp.bfloat16)


def combine(info, blocks, metas):
    meta_spec = pl.BlockSpec((BLOCK, META), lambda i: (0, HALF // META))
    return list(pl.pallas_call(
        combine_kernel,
        grid=(1,),
        out_shape=[jax.ShapeDtypeStruct((BLOCK, HALF), jnp.bfloat16)] * RING,
        in_specs=[SMEM_SPEC] + [VMEM_SPEC] * (2 * RING) + [meta_spec] * RING,
        out_specs=[VMEM_SPEC] * RING,
        compiler_params=pltpu.CompilerParams(vmem_limit_bytes=SMALL_VMEM),
        cost_estimate=pl.CostEstimate(
            flops=8 * RING * BLOCK * BLOCK * HALF, bytes_accessed=24 * BLOCK * HALF, transcendentals=0),
    )(info, *blocks, *metas))


def weight_copies(chunks, gate_hbm, up_hbm, w_in, in_sem):
    half = w_in.shape[1] // 2
    copies, at = [], 0
    for i, (col, size) in enumerate(chunks):
        col = pl.multiple_of(col, BLOCK)
        copies.append((
            pltpu.make_async_copy(gate_hbm.at[pl.ds(col, size)], w_in.at[pl.ds(at, size), pl.ds(0, half)],
                                  in_sem.at[2 * i]),
            pltpu.make_async_copy(up_hbm.at[pl.ds(col, size)], w_in.at[pl.ds(at, size), pl.ds(half, half)],
                                  in_sem.at[2 * i + 1])))
        at += size
    return copies


def block_copies(blocks, target, sems, first):
    return [pltpu.make_async_copy(blocks[r], target.at[pl.ds(r * BLOCK, BLOCK)], sems.at[first + r])
            for r in range(RING)]


def start_all(copies):
    for copy in copies:
        copy.start()


def wait_all(copies):
    for copy in copies:
        copy.wait()


def begin_kernel(info, pairs, tokens, picks, mix, mine, theirs):
    slot = picks[...]
    moved = slot < 0
    for i in range(pairs.shape[0]):
        for j in range(pairs.shape[1]):
            moved = moved | (slot == pairs[i, j])
    owner = jnp.where(moved, slot ^ 32, slot).astype(jnp.bfloat16)
    high = mix[...].astype(jnp.bfloat16)
    low = (mix[...] - high.astype(jnp.float32)).astype(jnp.bfloat16)
    meta = jnp.zeros((GROUP, META), jnp.float32)
    for i, part in enumerate((owner, high, low)):
        lane = iota((TOP, META), 1) == iota((TOP, META), 0) + i * TOP
        lane = jnp.where(lane, 1.0, 0.0).astype(jnp.bfloat16)
        meta += lax.dot_general(part, lane, (((0,), (0,)), ((), ())), preferred_element_type=jnp.float32)
    meta = meta.astype(jnp.bfloat16)
    mine[:, HALF:] = meta
    theirs[:, HALF:] = meta
    for core in range(CORES):
        @pl.when(info[0] == core)
        def _():
            mine[:, :HALF] = tokens[:, HALF * core:HALF * (core + 1)]
            theirs[:, :HALF] = tokens[:, HALF * (1 - core):HALF * (2 - core)]


def begin(info, pairs, tokens, picks, mix):
    out = jax.ShapeDtypeStruct((GROUP, HALF + META), jnp.bfloat16)
    return pl.pallas_call(
        begin_kernel,
        out_shape=[out, out],
        in_specs=[SMEM_SPEC, SMEM_SPEC] + [VMEM_SPEC] * 3,
        out_specs=[VMEM_SPEC, VMEM_SPEC],
        compiler_params=pltpu.CompilerParams(vmem_limit_bytes=SMALL_VMEM),
    )(info, pairs.T, tokens, picks.T, mix.T)


def project_kernel(info, *refs):
    blocks, (gate_hbm, up_hbm, total, x, w_in, x_sem, in_sem) = refs[:RING], refs[RING:]
    base = info[0] * HALF
    steps = column_chunks(HALF)
    x_copies = block_copies(blocks, x, x_sem, 0)
    in_copies = weight_copies([(base + start, size) for start, size in steps], gate_hbm, up_hbm, w_in, in_sem)
    start_all(x_copies)
    for pair in in_copies:
        start_all(pair)
    wait_all(x_copies)
    for (start, size), pair in zip(steps, in_copies):
        wait_all(pair)
        cols = slice(start, start + size)
        got = jnp.dot(x[:, cols], w_in[cols, :], preferred_element_type=jnp.float32)
        if start == 0:
            total[...] = got
        else:
            total[...] += got


def project(info, blocks, gate_w, up_w):
    rows, hid = RING * BLOCK, gate_w.shape[1]
    return pl.pallas_call(
        project_kernel,
        out_shape=jax.ShapeDtypeStruct((rows, 2 * hid), jnp.float32),
        in_specs=[SMEM_SPEC] + [HBM_SPEC] * 6,
        out_specs=VMEM_SPEC,
        scratch_shapes=[
            pltpu.VMEM((rows, HALF), jnp.bfloat16), pltpu.VMEM((HALF, 2 * hid), jnp.bfloat16),
            pltpu.SemaphoreType.DMA((RING,)), pltpu.SemaphoreType.DMA((2 * len(column_chunks(HALF)),)),
        ],
        compiler_params=pltpu.CompilerParams(vmem_limit_bytes=LARGE_VMEM),
        cost_estimate=pl.CostEstimate(
            flops=4 * rows * HALF * hid, bytes_accessed=2 * (2 * HALF * hid + rows * HALF), transcendentals=0),
    )(info, *blocks, gate_w, up_w)


def expert_kernel(info, *refs):
    near, far = refs[0], refs[1:1 + RING]
    gate_hbm, up_hbm, down_hbm = refs[5:8]
    main_outs, hidden_far = refs[8:12], refs[12]
    x, w_in, w_out, a1, a2, h1, h2, o, x_sem, in_sem, down_sem, out_sem = refs[13:]
    core = info[0]
    first = core == 0
    half = w_in.shape[1] // 2
    at_near, at_far = core * HALF, (1 - core) * HALF
    steps = column_chunks(HALF)
    far_copies = block_copies(far, x, x_sem, 0)
    near_copy = pltpu.make_async_copy(near, a1, x_sem.at[RING])
    in_copies = weight_copies([(at_far + start, size) for start, size in steps], gate_hbm, up_hbm, w_in, in_sem)
    down_copies = [pltpu.make_async_copy(
        down_hbm.at[:, pl.ds(pl.multiple_of(at_near + start, BLOCK), size)], w_out.at[:, pl.ds(start, size)],
        down_sem.at[i]) for i, (start, size) in enumerate(steps)]
    start_all(far_copies)
    for pair in in_copies:
        start_all(pair)
    near_copy.start()
    start_all(down_copies)

    wait_all(far_copies)
    for (start, size), pair in zip(steps, in_copies):
        wait_all(pair)
        cols = slice(start, start + size)
        got = jnp.dot(x[:, cols], w_in[cols, :], preferred_element_type=jnp.float32)
        if start == 0:
            a2[...] = got
        else:
            a2[...] += got
    near_copy.wait()

    def activate(i, carry):
        x, y, z = i // 16, i // 4 % 4, i % 4
        left, right = i, z * 16 + x * 4 + y
        i1 = pl.multiple_of(jnp.where(first, left, right) * 8, 8)
        i2 = pl.multiple_of(jnp.where(first, right, left) * 8, 8)
        both = a1[pl.ds(i1, 8)] + a2[pl.ds(i2, 8)]
        gate, up = both[:, :half], both[:, half:]
        value = gate / (1.0 + jnp.exp(-gate)) * up
        h1[pl.ds(i1, 8)] = value
        h2[pl.ds(i2, 8)] = value
        return carry

    lax.fori_loop(0, RING ** 3, activate, 0, unroll=4)
    hidden_far[...] = h2[...].astype(jnp.bfloat16)
    hidden = h1[...].astype(jnp.bfloat16)
    out_copies = []
    for i, ((start, size), copy) in enumerate(zip(steps, down_copies)):
        copy.wait()
        got = jnp.dot(hidden, w_out[:, start:start + size], preferred_element_type=jnp.float32)
        o[:, start:start + size] = got.astype(jnp.bfloat16)
        for r in range(RING):
            out_copies.append(pltpu.make_async_copy(
                o.at[pl.ds(r * BLOCK, BLOCK), pl.ds(start, size)],
                main_outs[r].at[:, pl.ds(start, size)], out_sem.at[RING * i + r]))
            out_copies[-1].start()
    wait_all(out_copies)


def expert(info, near, far, gate_w, up_w, down_w):
    rows, (width, hid) = RING * BLOCK, gate_w.shape
    steps = len(column_chunks(HALF))
    bf, f32 = jnp.bfloat16, jnp.float32
    out = pl.pallas_call(
        expert_kernel,
        out_shape=[jax.ShapeDtypeStruct((BLOCK, HALF), bf)] * RING + [jax.ShapeDtypeStruct((rows, hid), bf)],
        in_specs=[SMEM_SPEC] + [HBM_SPEC] * 8,
        out_specs=[HBM_SPEC] * RING + [VMEM_SPEC],
        scratch_shapes=[
            pltpu.VMEM((rows, HALF), bf), pltpu.VMEM((HALF, 2 * hid), bf), pltpu.VMEM((hid, HALF), bf),
            pltpu.VMEM((rows, 2 * hid), f32), pltpu.VMEM((rows, 2 * hid), f32),
            pltpu.VMEM((rows, hid), f32), pltpu.VMEM((rows, hid), f32),
            pltpu.VMEM((rows, HALF), bf),
            pltpu.SemaphoreType.DMA((RING + 1,)), pltpu.SemaphoreType.DMA((2 * steps,)),
            pltpu.SemaphoreType.DMA((steps,)), pltpu.SemaphoreType.DMA((RING * steps,)),
        ],
        compiler_params=pltpu.CompilerParams(vmem_limit_bytes=LARGE_VMEM),
        cost_estimate=pl.CostEstimate(
            flops=6 * rows * HALF * hid, bytes_accessed=2 * (3 * HALF * hid + 2 * rows * HALF),
            transcendentals=rows * hid),
    )(info, near, *far, gate_w, up_w, down_w)
    return list(out[:RING]), out[RING]


def spread_kernel(info, hidden, down_hbm, *refs):
    outs, (w_out, down_sem) = refs[:RING], refs[RING:]
    base = (1 - info[0]) * HALF
    steps = column_chunks(HALF)
    copies = [pltpu.make_async_copy(
        down_hbm.at[:, pl.ds(pl.multiple_of(base + start, BLOCK), size)], w_out.at[:, pl.ds(start, size)],
        down_sem.at[i]) for i, (start, size) in enumerate(steps)]
    start_all(copies)
    for (start, size), copy in zip(steps, copies):
        copy.wait()
        cols = slice(start, start + size)
        got = jnp.dot(hidden[...], w_out[:, cols], preferred_element_type=jnp.float32).astype(jnp.bfloat16)
        for r in range(RING):
            outs[r][:, cols] = got[BLOCK * r:BLOCK * (r + 1)]


def spread(info, hidden, down_w):
    rows, hid = hidden.shape
    out = pl.pallas_call(
        spread_kernel,
        out_shape=[jax.ShapeDtypeStruct((BLOCK, HALF), jnp.bfloat16)] * RING,
        in_specs=[SMEM_SPEC, VMEM_SPEC, HBM_SPEC],
        out_specs=[VMEM_SPEC] * RING,
        scratch_shapes=[
            pltpu.VMEM((hid, HALF), jnp.bfloat16), pltpu.SemaphoreType.DMA((len(column_chunks(HALF)),))],
        compiler_params=pltpu.CompilerParams(vmem_limit_bytes=LARGE_VMEM),
        cost_estimate=pl.CostEstimate(
            flops=2 * rows * HALF * hid, bytes_accessed=2 * HALF * (hid + rows), transcendentals=0),
    )(info, hidden, down_w)
    return list(out)


def summed(blocks):
    return sum(b.astype(jnp.float32) for b in blocks).astype(jnp.bfloat16)


def split_rows(value):
    return list(value.reshape(RING, -1, value.shape[-1]))


def per_device(tokens, picks, mix_weights, pairs, gate_weight, up_weight, down_weight):
    tok_rows, width = tokens.shape
    c = lax.axis_index("c")
    x = lax.axis_index("xh") * 2 + lax.axis_index("dp")
    z = lax.axis_index("z")
    y = lax.axis_index("y")
    first = c == 0

    shifts = jnp.array(SHIFTS, jnp.int32)
    place = lambda x, z, y: ((x // 2 * RING + z) * RING + y) * CORES + c + 0 * shifts
    along_x = place((x + shifts) % RING, z, y)
    along_z = place(x, (z + shifts) % RING, y)
    info = jnp.concatenate([jnp.stack([c, c, c, c]), jnp.where(first, along_x, along_z)]).astype(jnp.int32)

    mine, theirs = begin(info, pairs, tokens, picks, mix_weights)
    theirs = other_core(theirs)
    pool = jnp.where(first, jnp.concatenate([mine, theirs]), jnp.concatenate([theirs, mine]))
    pool = jnp.concatenate(gathered(pool, ROUTE[0]), axis=0)
    pool = gathered(pool, ROUTE[1])

    own, far = pack(info, pool, 0), pack(info, pool, 1)
    own = own[:1] + hop(own, ROUTE[2], ring_perm, (1, 2, 3))
    far = hop(far, ROUTE[2], ring_perm, (0, 1, 2, 3), cross=True)
    gate_w, up_w, down_w = gate_weight[0], up_weight[0], down_weight[0]
    near = project(info, own, gate_w, up_w)
    own, hidden = expert(info, near, far, gate_w, up_w, down_w)
    far = spread(info, hidden, down_w)
    own = own[:1] + hop(own, ROUTE[2], back_perm, (1, 2, 3))
    far = hop(far, ROUTE[2], back_perm, (0, 1, 2, 3), cross=True)
    sums = combine(info, own + far, pool)
    sums = summed(scattered(sums, ROUTE[1]))
    done = summed(scattered(split_rows(sums), ROUTE[0]))
    own = jnp.where(first, done[:tok_rows], done[tok_rows:])
    rest = other_core(jnp.where(first, done[tok_rows:], done[:tok_rows]))
    return jnp.where(first, jnp.concatenate([own, rest], axis=1), jnp.concatenate([rest, own], axis=1))


def solution(mesh):
    fine = Mesh(mesh.devices.reshape(2, 2, RING, RING, CORES), ALL_AXES)
    experts = ("xh", "z", "y", "c")
    return jax.shard_map(
        per_device,
        mesh=fine,
        in_specs=(
            P(ALL_AXES, None),
            P(ALL_AXES, None),
            P(ALL_AXES, None),
            P(),
            P(experts, None, "dp"),
            P(experts, None, "dp"),
            P(experts, "dp", None),
        ),
        out_specs=P(ALL_AXES, None),
        check_vma=False,
    )
```

```python
import functools
import itertools

import jax
import jax.numpy as jnp
from jax import lax
from jax.experimental import pallas as pl
from jax.experimental.pallas import tpu as pltpu
from jax.sharding import Mesh, PartitionSpec as P

ALL_AXES = ("dp", "xh", "z", "y", "c")
RING = 4
CORES = 2
CAP = 4
TOP = 8
GROUP = 16
META = 128
HALF = 3584
BLOCK = 128
SHIFTS = (0, 1, 3, 2)
ROUTE = (("y", "y"), ("z", "x"), ("x", "z"))
SMALL_VMEM = 24 << 20
LARGE_VMEM = 56 << 20
PROJECT_VMEM = 30 << 20
EXPERT_VMEM = 18 << 20


def flat_index(x, z, y, c):
    return ((((x % 2) * 2 + x // 2) * RING + z) * RING + y) * CORES + c


def ring_perm(axes, shift, cross=False):
    pairs = []
    for x, z, y, c in itertools.product(range(RING), range(RING), range(RING), range(CORES)):
        there = {"x": x, "z": z, "y": y}
        there[axes[c]] = (there[axes[c]] + shift) % RING
        target = flat_index(there["x"], there["z"], there["y"], 1 - c if cross else c)
        pairs.append((flat_index(x, z, y, c), target))
    return pairs


def together(*values):
    return lax.optimization_barrier(values)


def back_perm(axes, shift, cross=False):
    return [(target, source) for source, target in ring_perm(axes, shift, cross)]


def gathered(value, axes):
    return [value] + [lax.ppermute(value, ALL_AXES, ring_perm(axes, s)) for s in SHIFTS[1:]]


def scattered(blocks, axes):
    return [blocks[0]] + [lax.ppermute(b, ALL_AXES, back_perm(axes, s)) for b, s in zip(blocks[1:], SHIFTS[1:])]


def other_core(value):
    return lax.ppermute(value, "c", [(0, 1), (1, 0)])


def hop(blocks, axes, perm, numbers, cross=False):
    return [other_core(blocks[r]) if r == 0 else lax.ppermute(blocks[r], ALL_AXES, perm(axes, SHIFTS[r], cross))
            for r in numbers]


def column_chunks(width):
    steps, start = [], 0
    while start < width:
        size = min(1792, width - start)
        steps.append((start, size))
        start += size
    return steps


def iota(shape, dim):
    return lax.broadcasted_iota(jnp.int32, shape, dim)


def slots_of(meta, experts):
    turned = jnp.transpose(meta.astype(jnp.float32))
    owner = turned[:TOP]
    match = [owner == e.astype(jnp.float32) for e in experts]
    hits = [jnp.max(jnp.where(m, 1.0, 0.0), axis=0, keepdims=True) for m in match]
    stacked = jnp.concatenate(hits * (8 // len(hits)), axis=0)
    row, col = iota((BLOCK, BLOCK), 0), iota((BLOCK, BLOCK), 1)
    before = jnp.where((row // GROUP == col // GROUP) & (row < col), 1.0, 0.0)
    rank = jnp.dot(stacked.astype(jnp.bfloat16), before.astype(jnp.bfloat16),
                   preferred_element_type=jnp.float32)
    base = (iota((1, BLOCK), 1) // GROUP * CAP).astype(jnp.float32)
    slot = iota((BLOCK // RING, BLOCK), 0).astype(jnp.float32)
    place = [slot == jnp.where(h > 0.5, base + rank[e:e + 1], -1.0) for e, h in enumerate(hits)]
    return place, match, turned


def experts_at(info):
    own = [info[4 + r] for r in range(RING)]
    return own + [e ^ 1 for e in own]


def pack_kernel(cross, info, *refs):
    blocks, outs = refs[:RING], refs[RING:]
    experts = experts_at(info)[RING * cross:RING * cross + RING]
    rows = BLOCK // RING
    for b in range(RING):
        place, _, _ = slots_of(blocks[b][:, HALF:HALF + META], experts)
        spread = jnp.concatenate([jnp.where(p, 1.0, 0.0) for p in place], axis=0).astype(jnp.bfloat16)
        for start, size in column_chunks(HALF):
            cols = slice(start, start + size)
            got = jnp.dot(spread, blocks[b][:, cols], preferred_element_type=jnp.float32).astype(jnp.bfloat16)
            for e, out in enumerate(outs):
                out[rows * b:rows * (b + 1), cols] = got[rows * e:rows * (e + 1)]


VMEM_SPEC = pl.BlockSpec(memory_space=pltpu.VMEM)
SMEM_SPEC = pl.BlockSpec(memory_space=pltpu.SMEM)
HBM_SPEC = pl.BlockSpec(memory_space=pltpu.HBM)


def pack(info, blocks, cross):
    return list(pl.pallas_call(
        functools.partial(pack_kernel, cross),
        out_shape=[jax.ShapeDtypeStruct((BLOCK, HALF), jnp.bfloat16)] * RING,
        in_specs=[SMEM_SPEC] + [VMEM_SPEC] * RING,
        out_specs=[VMEM_SPEC] * RING,
        compiler_params=pltpu.CompilerParams(vmem_limit_bytes=SMALL_VMEM),
        cost_estimate=pl.CostEstimate(
            flops=2 * RING * BLOCK * BLOCK * HALF, bytes_accessed=16 * BLOCK * HALF, transcendentals=0),
    )(info, *blocks))


def combine_kernel(info, *refs):
    blocks, metas, outs = refs[:2 * RING], refs[2 * RING:3 * RING], refs[3 * RING:]
    experts = experts_at(info)
    rows = BLOCK // RING
    for b in range(RING):
        place, match, turned = slots_of(metas[b][...], experts)
        parts = []
        for offset in (TOP, 2 * TOP):
            mix = turned[offset:offset + TOP]
            picked = [jnp.sum(jnp.where(m, mix, 0.0), axis=0, keepdims=True) for m in match]
            weight = jnp.concatenate([jnp.where(p, w, 0.0) for p, w in zip(place, picked)], axis=0)
            parts.append(jnp.transpose(weight))
        mixer = jnp.concatenate(parts, axis=0).astype(jnp.bfloat16)
        for start, size in column_chunks(HALF):
            cols = slice(start, start + size)
            data = jnp.concatenate([block[rows * b:rows * (b + 1), cols] for block in blocks], axis=0)
            got = jnp.dot(mixer, data, preferred_element_type=jnp.float32)
            outs[b][:, cols] = (got[:BLOCK] + got[BLOCK:]).astype(jnp.bfloat16)


def combine(info, blocks, metas):
    meta_spec = pl.BlockSpec((BLOCK, META), lambda i: (0, HALF // META))
    return list(pl.pallas_call(
        combine_kernel,
        grid=(1,),
        out_shape=[jax.ShapeDtypeStruct((BLOCK, HALF), jnp.bfloat16)] * RING,
        in_specs=[SMEM_SPEC] + [VMEM_SPEC] * (2 * RING) + [meta_spec] * RING,
        out_specs=[VMEM_SPEC] * RING,
        compiler_params=pltpu.CompilerParams(vmem_limit_bytes=SMALL_VMEM),
        cost_estimate=pl.CostEstimate(
            flops=8 * RING * BLOCK * BLOCK * HALF, bytes_accessed=24 * BLOCK * HALF, transcendentals=0),
    )(info, *blocks, *metas))


def weight_copies(chunks, gate_hbm, up_hbm, w_in, in_sem):
    half = w_in.shape[1] // 2
    copies, at = [], 0
    for i, (col, size) in enumerate(chunks):
        col = pl.multiple_of(col, BLOCK)
        copies.append((
            pltpu.make_async_copy(gate_hbm.at[pl.ds(col, size)], w_in.at[pl.ds(at, size), pl.ds(0, half)],
                                  in_sem.at[2 * i]),
            pltpu.make_async_copy(up_hbm.at[pl.ds(col, size)], w_in.at[pl.ds(at, size), pl.ds(half, half)],
                                  in_sem.at[2 * i + 1])))
        at += size
    return copies


def block_copies(blocks, target, sems, first):
    return [pltpu.make_async_copy(blocks[r], target.at[pl.ds(r * BLOCK, BLOCK)], sems.at[first + r])
            for r in range(RING)]


def start_all(copies):
    for copy in copies:
        copy.start()


def wait_all(copies):
    for copy in copies:
        copy.wait()


def begin_kernel(info, pairs, tokens, picks, mix, mine, theirs):
    slot = picks[...]
    moved = slot < 0
    for i in range(pairs.shape[0]):
        for j in range(pairs.shape[1]):
            moved = moved | (slot == pairs[i, j])
    owner = jnp.where(moved, slot ^ 32, slot).astype(jnp.bfloat16)
    high = mix[...].astype(jnp.bfloat16)
    low = (mix[...] - high.astype(jnp.float32)).astype(jnp.bfloat16)
    meta = jnp.zeros((GROUP, META), jnp.float32)
    for i, part in enumerate((owner, high, low)):
        lane = iota((TOP, META), 1) == iota((TOP, META), 0) + i * TOP
        lane = jnp.where(lane, 1.0, 0.0).astype(jnp.bfloat16)
        meta += lax.dot_general(part, lane, (((0,), (0,)), ((), ())), preferred_element_type=jnp.float32)
    meta = meta.astype(jnp.bfloat16)
    mine[:, HALF:] = meta
    theirs[:, HALF:] = meta
    for core in range(CORES):
        @pl.when(info[0] == core)
        def _():
            mine[:, :HALF] = tokens[:, HALF * core:HALF * (core + 1)]
            theirs[:, :HALF] = tokens[:, HALF * (1 - core):HALF * (2 - core)]


def begin(info, pairs, tokens, picks, mix):
    out = jax.ShapeDtypeStruct((GROUP, HALF + META), jnp.bfloat16)
    return pl.pallas_call(
        begin_kernel,
        out_shape=[out, out],
        in_specs=[SMEM_SPEC, SMEM_SPEC] + [VMEM_SPEC] * 3,
        out_specs=[VMEM_SPEC, VMEM_SPEC],
        compiler_params=pltpu.CompilerParams(vmem_limit_bytes=SMALL_VMEM),
    )(info, pairs.T, tokens, picks.T, mix.T)


def project_kernel(info, *refs):
    blocks, (gate_hbm, up_hbm, down_hbm), (total, w_far, w_out) = refs[:RING], refs[RING:RING + 3], refs[RING + 3:RING + 6]
    x, w_in, x_sem, in_sem, far_sem, down_sem = refs[RING + 6:]
    at_near, at_far = info[0] * HALF, (1 - info[0]) * HALF
    steps = column_chunks(HALF)
    x_copies = block_copies(blocks, x, x_sem, 0)
    in_copies = weight_copies([(at_near + start, size) for start, size in steps], gate_hbm, up_hbm, w_in, in_sem)
    far_copies = weight_copies([(at_far, HALF)], gate_hbm, up_hbm, w_far, far_sem)[0]
    down_copy = pltpu.make_async_copy(
        down_hbm.at[:, pl.ds(pl.multiple_of(at_near, BLOCK), HALF)], w_out, down_sem)
    start_all(x_copies)
    for pair in in_copies:
        start_all(pair)
    start_all(far_copies)
    down_copy.start()
    wait_all(x_copies)
    for (start, size), pair in zip(steps, in_copies):
        wait_all(pair)
        cols = slice(start, start + size)
        got = jnp.dot(x[:, cols], w_in[cols, :], preferred_element_type=jnp.float32)
        if start == 0:
            total[...] = got
        else:
            total[...] += got
    wait_all(far_copies)
    down_copy.wait()


def project(info, blocks, gate_w, up_w, down_w):
    rows, hid = RING * BLOCK, gate_w.shape[1]
    bf = jnp.bfloat16
    return pl.pallas_call(
        project_kernel,
        out_shape=[jax.ShapeDtypeStruct((rows, 2 * hid), jnp.float32),
                   jax.ShapeDtypeStruct((HALF, 2 * hid), bf), jax.ShapeDtypeStruct((hid, HALF), bf)],
        in_specs=[SMEM_SPEC] + [HBM_SPEC] * 7,
        out_specs=[VMEM_SPEC] * 3,
        scratch_shapes=[
            pltpu.VMEM((rows, HALF), bf), pltpu.VMEM((HALF, 2 * hid), bf),
            pltpu.SemaphoreType.DMA((RING,)), pltpu.SemaphoreType.DMA((2 * len(column_chunks(HALF)),)),
            pltpu.SemaphoreType.DMA((2,)), pltpu.SemaphoreType.DMA,
        ],
        compiler_params=pltpu.CompilerParams(vmem_limit_bytes=PROJECT_VMEM),
        cost_estimate=pl.CostEstimate(
            flops=4 * rows * HALF * hid, bytes_accessed=2 * (5 * HALF * hid + rows * HALF), transcendentals=0),
    )(info, *blocks, gate_w, up_w, down_w)


def expert_kernel(info, near, w_in, w_out, *refs):
    far, main_outs, hidden_far = refs[:RING], refs[RING:2 * RING], refs[2 * RING]
    x, a2, h1, h2, o, x_sem, out_sem = refs[2 * RING + 1:]
    first = info[0] == 0
    half = w_in.shape[1] // 2
    steps = column_chunks(HALF)
    far_copies = [
        [pltpu.make_async_copy(
            far[r].at[:, pl.ds(start, size)], x.at[pl.ds(r * BLOCK, BLOCK), pl.ds(start, size)],
            x_sem.at[RING * i + r]) for r in range(RING)]
        for i, (start, size) in enumerate(steps)]
    for copies in far_copies:
        start_all(copies)
    for (start, size), copies in zip(steps, far_copies):
        wait_all(copies)
        cols = slice(start, start + size)
        got = jnp.dot(x[:, cols], w_in[cols, :], preferred_element_type=jnp.float32)
        if start == 0:
            a2[...] = got
        else:
            a2[...] += got

    rows = BLOCK // RING

    def activate(i, carry):
        left, right = i, i % RING * RING + i // RING
        i1 = pl.multiple_of(jnp.where(first, left, right) * rows, rows)
        i2 = pl.multiple_of(jnp.where(first, right, left) * rows, rows)
        both = near[pl.ds(i1, rows)] + a2[pl.ds(i2, rows)]
        gate, up = both[:, :half], both[:, half:]
        value = gate / (1.0 + jnp.exp(-gate)) * up
        h1[pl.ds(i1, rows)] = value
        h2[pl.ds(i2, rows)] = value
        return carry

    lax.fori_loop(0, RING ** 2, activate, 0)
    hidden_far[...] = h2[...].astype(jnp.bfloat16)
    hidden = h1[...].astype(jnp.bfloat16)
    out_copies = []
    for i, (start, size) in enumerate(steps):
        got = jnp.dot(hidden, w_out[:, start:start + size], preferred_element_type=jnp.float32)
        o[:, start:start + size] = got.astype(jnp.bfloat16)
        for r in range(RING):
            out_copies.append(pltpu.make_async_copy(
                o.at[pl.ds(r * BLOCK, BLOCK), pl.ds(start, size)],
                main_outs[r].at[:, pl.ds(start, size)], out_sem.at[RING * i + r]))
            out_copies[-1].start()
    wait_all(out_copies)


def expert(info, near, w_in, w_out, far):
    rows, hid = RING * BLOCK, w_out.shape[0]
    steps = len(column_chunks(HALF))
    bf, f32 = jnp.bfloat16, jnp.float32
    out = pl.pallas_call(
        expert_kernel,
        out_shape=[jax.ShapeDtypeStruct((BLOCK, HALF), bf)] * RING + [jax.ShapeDtypeStruct((rows, hid), bf)],
        in_specs=[SMEM_SPEC] + [VMEM_SPEC] * 3 + [HBM_SPEC] * RING,
        out_specs=[HBM_SPEC] * RING + [VMEM_SPEC],
        scratch_shapes=[
            pltpu.VMEM((rows, HALF), bf), pltpu.VMEM((rows, 2 * hid), f32),
            pltpu.VMEM((rows, hid), f32), pltpu.VMEM((rows, hid), f32), pltpu.VMEM((rows, HALF), bf),
            pltpu.SemaphoreType.DMA((RING * steps,)), pltpu.SemaphoreType.DMA((RING * steps,)),
        ],
        compiler_params=pltpu.CompilerParams(vmem_limit_bytes=EXPERT_VMEM),
        cost_estimate=pl.CostEstimate(
            flops=6 * rows * HALF * hid, bytes_accessed=4 * rows * HALF, transcendentals=rows * hid),
    )(info, near, w_in, w_out, *far)
    return list(out[:RING]), out[RING]


def spread_kernel(info, hidden, down_hbm, *refs):
    outs, (w_out, down_sem) = refs[:RING], refs[RING:]
    base = (1 - info[0]) * HALF
    steps = column_chunks(HALF)
    copies = [pltpu.make_async_copy(
        down_hbm.at[:, pl.ds(pl.multiple_of(base + start, BLOCK), size)], w_out.at[:, pl.ds(start, size)],
        down_sem.at[i]) for i, (start, size) in enumerate(steps)]
    start_all(copies)
    for (start, size), copy in zip(steps, copies):
        copy.wait()
        cols = slice(start, start + size)
        got = jnp.dot(hidden[...], w_out[:, cols], preferred_element_type=jnp.float32).astype(jnp.bfloat16)
        for r in range(RING):
            outs[r][:, cols] = got[BLOCK * r:BLOCK * (r + 1)]


def spread(info, hidden, down_w):
    rows, hid = hidden.shape
    out = pl.pallas_call(
        spread_kernel,
        out_shape=[jax.ShapeDtypeStruct((BLOCK, HALF), jnp.bfloat16)] * RING,
        in_specs=[SMEM_SPEC, VMEM_SPEC, HBM_SPEC],
        out_specs=[VMEM_SPEC] * RING,
        scratch_shapes=[
            pltpu.VMEM((hid, HALF), jnp.bfloat16), pltpu.SemaphoreType.DMA((len(column_chunks(HALF)),))],
        compiler_params=pltpu.CompilerParams(vmem_limit_bytes=LARGE_VMEM),
        cost_estimate=pl.CostEstimate(
            flops=2 * rows * HALF * hid, bytes_accessed=2 * HALF * (hid + rows), transcendentals=0),
    )(info, hidden, down_w)
    return list(out)


def summed(blocks):
    return sum(b.astype(jnp.float32) for b in blocks).astype(jnp.bfloat16)


def split_rows(value):
    return list(value.reshape(RING, -1, value.shape[-1]))


def per_device(tokens, picks, mix_weights, pairs, gate_weight, up_weight, down_weight):
    tok_rows, width = tokens.shape
    c = lax.axis_index("c")
    x = lax.axis_index("xh") * 2 + lax.axis_index("dp")
    z = lax.axis_index("z")
    y = lax.axis_index("y")
    first = c == 0

    shifts = jnp.array(SHIFTS, jnp.int32)
    place = lambda x, z, y: ((x // 2 * RING + z) * RING + y) * CORES + c + 0 * shifts
    along_x = place((x + shifts) % RING, z, y)
    along_z = place(x, (z + shifts) % RING, y)
    info = jnp.concatenate([jnp.stack([c, c, c, c]), jnp.where(first, along_x, along_z)]).astype(jnp.int32)

    mine, theirs = begin(info, pairs, tokens, picks, mix_weights)
    theirs = other_core(theirs)
    pool = jnp.where(first, jnp.concatenate([mine, theirs]), jnp.concatenate([theirs, mine]))
    line, part = together(gathered(pool, ROUTE[0]), lax.ppermute(pool, ALL_AXES, ring_perm(ROUTE[1], SHIFTS[3])))
    line = jnp.concatenate(line, axis=0)
    ahead, part = together(hop([line] * RING, ROUTE[1], ring_perm, (1, 2)), gathered(part, ROUTE[0]))
    pool = [line] + ahead + [jnp.concatenate(part, axis=0)]

    own, far = pack(info, pool, 0), pack(info, pool, 1)
    own = own[:1] + hop(own, ROUTE[2], ring_perm, (1, 2, 3))
    far = hop(far, ROUTE[2], ring_perm, (0, 1, 2, 3), cross=True)
    gate_w, up_w, down_w = gate_weight[0], up_weight[0], down_weight[0]
    near, w_in, w_out = project(info, own, gate_w, up_w, down_w)
    own, hidden = expert(info, near, w_in, w_out, far)
    far = spread(info, hidden, down_w)
    own = own[:1] + hop(own, ROUTE[2], back_perm, (1, 2, 3))
    far = hop(far, ROUTE[2], back_perm, (0, 1, 2, 3), cross=True)
    sums = combine(info, own + far, pool)
    ahead, part = together(hop(sums, ROUTE[1], back_perm, (1, 2)), scattered(split_rows(sums[3]), ROUTE[0]))
    line, part = summed(sums[:1] + ahead), summed(part)
    line, part = together(
        scattered(split_rows(line), ROUTE[0]), lax.ppermute(part, ALL_AXES, back_perm(ROUTE[1], SHIFTS[3])))
    done = summed(line + [part])
    own = jnp.where(first, done[:tok_rows], done[tok_rows:])
    rest = other_core(jnp.where(first, done[tok_rows:], done[:tok_rows]))
    return jnp.where(first, jnp.concatenate([own, rest], axis=1), jnp.concatenate([rest, own], axis=1))


def solution(mesh):
    fine = Mesh(mesh.devices.reshape(2, 2, RING, RING, CORES), ALL_AXES)
    experts = ("xh", "z", "y", "c")
    return jax.shard_map(
        per_device,
        mesh=fine,
        in_specs=(
            P(ALL_AXES, None),
            P(ALL_AXES, None),
            P(ALL_AXES, None),
            P(),
            P(experts, None, "dp"),
            P(experts, None, "dp"),
            P(experts, "dp", None),
        ),
        out_specs=P(ALL_AXES, None),
        check_vma=False,
    )
```

```python
import functools
import itertools

import jax
import jax.numpy as jnp
from jax import lax
from jax.experimental import pallas as pl
from jax.experimental.pallas import tpu as pltpu
from jax.sharding import Mesh, PartitionSpec as P

ALL_AXES = ("dp", "xh", "z", "y", "c")
RING = 4
CORES = 2
CAP = 4
TOP = 8
GROUP = 16
META = 128
HALF = 3584
BLOCK = 128
SHIFTS = (0, 1, 3, 2)
ROUTE = (("y", "y"), ("z", "x"), ("x", "z"))
SMALL_VMEM = 24 << 20
LARGE_VMEM = 56 << 20
PROJECT_VMEM = 30 << 20
EXPERT_VMEM = 18 << 20


def flat_index(x, z, y, c):
    return ((((x % 2) * 2 + x // 2) * RING + z) * RING + y) * CORES + c


def ring_perm(axes, shift, cross=False):
    pairs = []
    for x, z, y, c in itertools.product(range(RING), range(RING), range(RING), range(CORES)):
        there = {"x": x, "z": z, "y": y}
        there[axes[c]] = (there[axes[c]] + shift) % RING
        target = flat_index(there["x"], there["z"], there["y"], 1 - c if cross else c)
        pairs.append((flat_index(x, z, y, c), target))
    return pairs


def together(*values):
    return lax.optimization_barrier(values)


def back_perm(axes, shift, cross=False):
    return [(target, source) for source, target in ring_perm(axes, shift, cross)]


def gathered(value, axes):
    return [value] + [lax.ppermute(value, ALL_AXES, ring_perm(axes, s)) for s in SHIFTS[1:]]


def scattered(blocks, axes):
    return [blocks[0]] + [lax.ppermute(b, ALL_AXES, back_perm(axes, s)) for b, s in zip(blocks[1:], SHIFTS[1:])]


def other_core(value):
    return lax.ppermute(value, "c", [(0, 1), (1, 0)])


def hop(blocks, axes, perm, numbers, cross=False):
    return [other_core(blocks[r]) if r == 0 else lax.ppermute(blocks[r], ALL_AXES, perm(axes, SHIFTS[r], cross))
            for r in numbers]


def column_chunks(width):
    steps, start = [], 0
    while start < width:
        size = min(1792, width - start)
        steps.append((start, size))
        start += size
    return steps


def iota(shape, dim):
    return lax.broadcasted_iota(jnp.int32, shape, dim)


def slots_of(meta, experts):
    turned = jnp.transpose(meta.astype(jnp.float32))
    owner = turned[:TOP]
    match = [owner == e.astype(jnp.float32) for e in experts]
    hits = [jnp.max(jnp.where(m, 1.0, 0.0), axis=0, keepdims=True) for m in match]
    stacked = jnp.concatenate(hits * (8 // len(hits)), axis=0)
    row, col = iota((BLOCK, BLOCK), 0), iota((BLOCK, BLOCK), 1)
    before = jnp.where((row // GROUP == col // GROUP) & (row < col), 1.0, 0.0)
    rank = jnp.dot(stacked.astype(jnp.bfloat16), before.astype(jnp.bfloat16),
                   preferred_element_type=jnp.float32)
    base = (iota((1, BLOCK), 1) // GROUP * CAP).astype(jnp.float32)
    slot = iota((BLOCK // RING, BLOCK), 0).astype(jnp.float32)
    place = [slot == jnp.where(h > 0.5, base + rank[e:e + 1], -1.0) for e, h in enumerate(hits)]
    return place, match, turned


def experts_at(info):
    own = [info[4 + r] for r in range(RING)]
    return own + [e ^ 1 for e in own]


def pack_kernel(cross, info, *refs):
    blocks, outs = refs[:RING], refs[RING:]
    experts = experts_at(info)[RING * cross:RING * cross + RING]
    rows = BLOCK // RING
    for b in range(RING):
        place, _, _ = slots_of(blocks[b][:, HALF:HALF + META], experts)
        spread = jnp.concatenate([jnp.where(p, 1.0, 0.0) for p in place], axis=0).astype(jnp.bfloat16)
        for start, size in column_chunks(HALF):
            cols = slice(start, start + size)
            got = jnp.dot(spread, blocks[b][:, cols], preferred_element_type=jnp.float32).astype(jnp.bfloat16)
            for e, out in enumerate(outs):
                out[rows * b:rows * (b + 1), cols] = got[rows * e:rows * (e + 1)]


VMEM_SPEC = pl.BlockSpec(memory_space=pltpu.VMEM)
SMEM_SPEC = pl.BlockSpec(memory_space=pltpu.SMEM)
HBM_SPEC = pl.BlockSpec(memory_space=pltpu.HBM)


def pack(info, blocks, cross):
    return list(pl.pallas_call(
        functools.partial(pack_kernel, cross),
        out_shape=[jax.ShapeDtypeStruct((BLOCK, HALF), jnp.bfloat16)] * RING,
        in_specs=[SMEM_SPEC] + [VMEM_SPEC] * RING,
        out_specs=[VMEM_SPEC] * RING,
        compiler_params=pltpu.CompilerParams(vmem_limit_bytes=SMALL_VMEM),
        cost_estimate=pl.CostEstimate(
            flops=2 * RING * BLOCK * BLOCK * HALF, bytes_accessed=16 * BLOCK * HALF, transcendentals=0),
    )(info, *blocks))


def combine_kernel(info, *refs):
    blocks, metas, outs = refs[:2 * RING], refs[2 * RING:3 * RING], refs[3 * RING:]
    experts = experts_at(info)
    rows = BLOCK // RING
    for b in range(RING):
        place, match, turned = slots_of(metas[b][...], experts)
        parts = []
        for offset in (TOP, 2 * TOP):
            mix = turned[offset:offset + TOP]
            picked = [jnp.sum(jnp.where(m, mix, 0.0), axis=0, keepdims=True) for m in match]
            weight = jnp.concatenate([jnp.where(p, w, 0.0) for p, w in zip(place, picked)], axis=0)
            parts.append(jnp.transpose(weight))
        mixer = jnp.concatenate(parts, axis=0).astype(jnp.bfloat16)
        for start, size in column_chunks(HALF):
            cols = slice(start, start + size)
            data = jnp.concatenate([block[rows * b:rows * (b + 1), cols] for block in blocks], axis=0)
            got = jnp.dot(mixer, data, preferred_element_type=jnp.float32)
            outs[b][:, cols] = (got[:BLOCK] + got[BLOCK:]).astype(jnp.bfloat16)


def combine(info, blocks, metas):
    meta_spec = pl.BlockSpec((BLOCK, META), lambda i: (0, HALF // META))
    return list(pl.pallas_call(
        combine_kernel,
        grid=(1,),
        out_shape=[jax.ShapeDtypeStruct((BLOCK, HALF), jnp.bfloat16)] * RING,
        in_specs=[SMEM_SPEC] + [VMEM_SPEC] * (2 * RING) + [meta_spec] * RING,
        out_specs=[VMEM_SPEC] * RING,
        compiler_params=pltpu.CompilerParams(vmem_limit_bytes=SMALL_VMEM),
        cost_estimate=pl.CostEstimate(
            flops=8 * RING * BLOCK * BLOCK * HALF, bytes_accessed=24 * BLOCK * HALF, transcendentals=0),
    )(info, *blocks, *metas))


def weight_copies(chunks, gate_hbm, up_hbm, w_in, in_sem):
    half = w_in.shape[1] // 2
    copies, at = [], 0
    for i, (col, size) in enumerate(chunks):
        col = pl.multiple_of(col, BLOCK)
        copies.append((
            pltpu.make_async_copy(gate_hbm.at[pl.ds(col, size)], w_in.at[pl.ds(at, size), pl.ds(0, half)],
                                  in_sem.at[2 * i]),
            pltpu.make_async_copy(up_hbm.at[pl.ds(col, size)], w_in.at[pl.ds(at, size), pl.ds(half, half)],
                                  in_sem.at[2 * i + 1])))
        at += size
    return copies


def block_copies(blocks, target, sems, first):
    return [pltpu.make_async_copy(blocks[r], target.at[pl.ds(r * BLOCK, BLOCK)], sems.at[first + r])
            for r in range(RING)]


def start_all(copies):
    for copy in copies:
        copy.start()


def wait_all(copies):
    for copy in copies:
        copy.wait()


def begin_kernel(info, pairs, tokens, picks, mix, mine, theirs):
    slot = picks[...]
    moved = slot < 0
    for i in range(pairs.shape[0]):
        for j in range(pairs.shape[1]):
            moved = moved | (slot == pairs[i, j])
    owner = jnp.where(moved, slot ^ 32, slot).astype(jnp.bfloat16)
    high = mix[...].astype(jnp.bfloat16)
    low = (mix[...] - high.astype(jnp.float32)).astype(jnp.bfloat16)
    meta = jnp.zeros((GROUP, META), jnp.float32)
    for i, part in enumerate((owner, high, low)):
        lane = iota((TOP, META), 1) == iota((TOP, META), 0) + i * TOP
        lane = jnp.where(lane, 1.0, 0.0).astype(jnp.bfloat16)
        meta += lax.dot_general(part, lane, (((0,), (0,)), ((), ())), preferred_element_type=jnp.float32)
    meta = meta.astype(jnp.bfloat16)
    mine[:, HALF:] = meta
    theirs[:, HALF:] = meta
    for core in range(CORES):
        @pl.when(info[0] == core)
        def _():
            mine[:, :HALF] = tokens[:, HALF * core:HALF * (core + 1)]
            theirs[:, :HALF] = tokens[:, HALF * (1 - core):HALF * (2 - core)]


def begin(info, pairs, tokens, picks, mix):
    out = jax.ShapeDtypeStruct((GROUP, HALF + META), jnp.bfloat16)
    return pl.pallas_call(
        begin_kernel,
        out_shape=[out, out],
        in_specs=[SMEM_SPEC, SMEM_SPEC] + [VMEM_SPEC] * 3,
        out_specs=[VMEM_SPEC, VMEM_SPEC],
        compiler_params=pltpu.CompilerParams(vmem_limit_bytes=SMALL_VMEM),
    )(info, pairs.T, tokens, picks.T, mix.T)


def project_kernel(info, *refs):
    blocks, (gate_hbm, up_hbm, down_hbm), (total, w_far, w_out) = refs[:RING], refs[RING:RING + 3], refs[RING + 3:RING + 6]
    x, w_in, x_sem, in_sem, far_sem, down_sem = refs[RING + 6:]
    at_near, at_far = info[0] * HALF, (1 - info[0]) * HALF
    steps = column_chunks(HALF)
    x_copies = block_copies(blocks, x, x_sem, 0)
    in_copies = weight_copies([(at_near + start, size) for start, size in steps], gate_hbm, up_hbm, w_in, in_sem)
    far_copies = weight_copies([(at_far, HALF)], gate_hbm, up_hbm, w_far, far_sem)[0]
    down_copy = pltpu.make_async_copy(
        down_hbm.at[:, pl.ds(pl.multiple_of(at_near, BLOCK), HALF)], w_out, down_sem)
    start_all(x_copies)
    for pair in in_copies:
        start_all(pair)
    start_all(far_copies)
    down_copy.start()
    wait_all(x_copies)
    for (start, size), pair in zip(steps, in_copies):
        wait_all(pair)
        cols = slice(start, start + size)
        got = jnp.dot(x[:, cols], w_in[cols, :], preferred_element_type=jnp.float32)
        if start == 0:
            total[...] = got
        else:
            total[...] += got
    wait_all(far_copies)
    down_copy.wait()


def project(info, blocks, gate_w, up_w, down_w):
    rows, hid = RING * BLOCK, gate_w.shape[1]
    bf = jnp.bfloat16
    return pl.pallas_call(
        project_kernel,
        out_shape=[jax.ShapeDtypeStruct((rows, 2 * hid), jnp.float32),
                   jax.ShapeDtypeStruct((HALF, 2 * hid), bf), jax.ShapeDtypeStruct((hid, HALF), bf)],
        in_specs=[SMEM_SPEC] + [HBM_SPEC] * 7,
        out_specs=[VMEM_SPEC] * 3,
        scratch_shapes=[
            pltpu.VMEM((rows, HALF), bf), pltpu.VMEM((HALF, 2 * hid), bf),
            pltpu.SemaphoreType.DMA((RING,)), pltpu.SemaphoreType.DMA((2 * len(column_chunks(HALF)),)),
            pltpu.SemaphoreType.DMA((2,)), pltpu.SemaphoreType.DMA,
        ],
        compiler_params=pltpu.CompilerParams(vmem_limit_bytes=PROJECT_VMEM),
        cost_estimate=pl.CostEstimate(
            flops=4 * rows * HALF * hid, bytes_accessed=2 * (5 * HALF * hid + rows * HALF), transcendentals=0),
    )(info, *blocks, gate_w, up_w, down_w)


def expert_kernel(info, near, w_in, w_out, *refs):
    far, main_outs, hidden_far = refs[:RING], refs[RING:2 * RING], refs[2 * RING]
    x, a2, h1, h2, o, x_sem, out_sem = refs[2 * RING + 1:]
    first = info[0] == 0
    half = w_in.shape[1] // 2
    steps = column_chunks(HALF)
    far_copies = [
        [pltpu.make_async_copy(
            far[r].at[:, pl.ds(start, size)], x.at[pl.ds(r * BLOCK, BLOCK), pl.ds(start, size)],
            x_sem.at[RING * i + r]) for r in range(RING)]
        for i, (start, size) in enumerate(steps)]
    for copies in far_copies:
        start_all(copies)
    for (start, size), copies in zip(steps, far_copies):
        wait_all(copies)
        cols = slice(start, start + size)
        got = jnp.dot(x[:, cols], w_in[cols, :], preferred_element_type=jnp.float32)
        if start == 0:
            a2[...] = got
        else:
            a2[...] += got

    rows = BLOCK // RING

    def activate(i, carry):
        left, right = i, i % RING * RING + i // RING
        i1 = pl.multiple_of(jnp.where(first, left, right) * rows, rows)
        i2 = pl.multiple_of(jnp.where(first, right, left) * rows, rows)
        both = near[pl.ds(i1, rows)] + a2[pl.ds(i2, rows)]
        gate, up = both[:, :half], both[:, half:]
        value = gate / (1.0 + jnp.exp(-gate)) * up
        h1[pl.ds(i1, rows)] = value
        h2[pl.ds(i2, rows)] = value
        return carry

    lax.fori_loop(0, RING ** 2, activate, 0)
    hidden_far[...] = h2[...].astype(jnp.bfloat16)
    hidden = h1[...].astype(jnp.bfloat16)
    out_copies = []
    for i, (start, size) in enumerate(steps):
        got = jnp.dot(hidden, w_out[:, start:start + size], preferred_element_type=jnp.float32)
        o[:, start:start + size] = got.astype(jnp.bfloat16)
        for r in range(RING):
            out_copies.append(pltpu.make_async_copy(
                o.at[pl.ds(r * BLOCK, BLOCK), pl.ds(start, size)],
                main_outs[r].at[:, pl.ds(start, size)], out_sem.at[RING * i + r]))
            out_copies[-1].start()
    wait_all(out_copies)


def expert(info, near, w_in, w_out, far):
    rows, hid = RING * BLOCK, w_out.shape[0]
    steps = len(column_chunks(HALF))
    bf, f32 = jnp.bfloat16, jnp.float32
    out = pl.pallas_call(
        expert_kernel,
        out_shape=[jax.ShapeDtypeStruct((BLOCK, HALF), bf)] * RING + [jax.ShapeDtypeStruct((rows, hid), bf)],
        in_specs=[SMEM_SPEC] + [VMEM_SPEC] * 3 + [HBM_SPEC] * RING,
        out_specs=[HBM_SPEC] * RING + [VMEM_SPEC],
        scratch_shapes=[
            pltpu.VMEM((rows, HALF), bf), pltpu.VMEM((rows, 2 * hid), f32),
            pltpu.VMEM((rows, hid), f32), pltpu.VMEM((rows, hid), f32), pltpu.VMEM((rows, HALF), bf),
            pltpu.SemaphoreType.DMA((RING * steps,)), pltpu.SemaphoreType.DMA((RING * steps,)),
        ],
        compiler_params=pltpu.CompilerParams(vmem_limit_bytes=EXPERT_VMEM),
        cost_estimate=pl.CostEstimate(
            flops=6 * rows * HALF * hid, bytes_accessed=4 * rows * HALF, transcendentals=rows * hid),
    )(info, near, w_in, w_out, *far)
    return list(out[:RING]), out[RING]


def spread_kernel(info, hidden, down_hbm, *refs):
    outs, (w_out, down_sem) = refs[:RING], refs[RING:]
    base = (1 - info[0]) * HALF
    steps = column_chunks(HALF)
    copies = [pltpu.make_async_copy(
        down_hbm.at[:, pl.ds(pl.multiple_of(base + start, BLOCK), size)], w_out.at[:, pl.ds(start, size)],
        down_sem.at[i]) for i, (start, size) in enumerate(steps)]
    start_all(copies)
    for (start, size), copy in zip(steps, copies):
        copy.wait()
        cols = slice(start, start + size)
        got = jnp.dot(hidden[...], w_out[:, cols], preferred_element_type=jnp.float32).astype(jnp.bfloat16)
        for r in range(RING):
            outs[r][:, cols] = got[BLOCK * r:BLOCK * (r + 1)]


def spread(info, hidden, down_w):
    rows, hid = hidden.shape
    out = pl.pallas_call(
        spread_kernel,
        out_shape=[jax.ShapeDtypeStruct((BLOCK, HALF), jnp.bfloat16)] * RING,
        in_specs=[SMEM_SPEC, VMEM_SPEC, HBM_SPEC],
        out_specs=[VMEM_SPEC] * RING,
        scratch_shapes=[
            pltpu.VMEM((hid, HALF), jnp.bfloat16), pltpu.SemaphoreType.DMA((len(column_chunks(HALF)),))],
        compiler_params=pltpu.CompilerParams(vmem_limit_bytes=LARGE_VMEM),
        cost_estimate=pl.CostEstimate(
            flops=2 * rows * HALF * hid, bytes_accessed=2 * HALF * (hid + rows), transcendentals=0),
    )(info, hidden, down_w)
    return list(out)


def summed(blocks):
    return sum(b.astype(jnp.float32) for b in blocks).astype(jnp.bfloat16)


def split_rows(value):
    return list(value.reshape(RING, -1, value.shape[-1]))


def per_device(tokens, picks, mix_weights, pairs, gate_weight, up_weight, down_weight):
    tok_rows, width = tokens.shape
    c = lax.axis_index("c")
    x = lax.axis_index("xh") * 2 + lax.axis_index("dp")
    z = lax.axis_index("z")
    y = lax.axis_index("y")
    first = c == 0

    shifts = jnp.array(SHIFTS, jnp.int32)
    place = lambda x, z, y: ((x // 2 * RING + z) * RING + y) * CORES + c + 0 * shifts
    along_x = place((x + shifts) % RING, z, y)
    along_z = place(x, (z + shifts) % RING, y)
    info = jnp.concatenate([jnp.stack([c, c, c, c]), jnp.where(first, along_x, along_z)]).astype(jnp.int32)

    mine, theirs = begin(info, pairs, tokens, picks, mix_weights)
    theirs = other_core(theirs)
    pool = jnp.where(first, jnp.concatenate([mine, theirs]), jnp.concatenate([theirs, mine]))
    part, line = together(lax.ppermute(pool, ALL_AXES, ring_perm(ROUTE[1], SHIFTS[3])), gathered(pool, ROUTE[0]))
    line = jnp.concatenate(line, axis=0)
    ahead, part = together(hop([line] * RING, ROUTE[1], ring_perm, (1, 2)), gathered(part, ROUTE[0]))
    pool = [line] + ahead + [jnp.concatenate(part, axis=0)]

    own, far = pack(info, pool, 0), pack(info, pool, 1)
    own = own[:1] + hop(own, ROUTE[2], ring_perm, (1, 2, 3))
    far = hop(far, ROUTE[2], ring_perm, (0, 1, 2, 3), cross=True)
    gate_w, up_w, down_w = gate_weight[0], up_weight[0], down_weight[0]
    near, w_in, w_out = project(info, own, gate_w, up_w, down_w)
    own, hidden = expert(info, near, w_in, w_out, far)
    far = spread(info, hidden, down_w)
    own = own[:1] + hop(own, ROUTE[2], back_perm, (1, 2, 3))
    far = hop(far, ROUTE[2], back_perm, (0, 1, 2, 3), cross=True)
    sums = combine(info, own + far, pool)
    ahead, part = together(hop(sums, ROUTE[1], back_perm, (1, 2)), scattered(split_rows(sums[3]), ROUTE[0]))
    line, part = summed(sums[:1] + ahead), summed(part)
    part, line = together(
        lax.ppermute(part, ALL_AXES, back_perm(ROUTE[1], SHIFTS[3])), scattered(split_rows(line), ROUTE[0]))
    done = summed(line + [part])
    own = jnp.where(first, done[:tok_rows], done[tok_rows:])
    rest = other_core(jnp.where(first, done[tok_rows:], done[:tok_rows]))
    return jnp.where(first, jnp.concatenate([own, rest], axis=1), jnp.concatenate([rest, own], axis=1))


def solution(mesh):
    fine = Mesh(mesh.devices.reshape(2, 2, RING, RING, CORES), ALL_AXES)
    experts = ("xh", "z", "y", "c")
    return jax.shard_map(
        per_device,
        mesh=fine,
        in_specs=(
            P(ALL_AXES, None),
            P(ALL_AXES, None),
            P(ALL_AXES, None),
            P(),
            P(experts, None, "dp"),
            P(experts, None, "dp"),
            P(experts, "dp", None),
        ),
        out_specs=P(ALL_AXES, None),
        check_vma=False,
    )
```

```python
import functools
import itertools

import jax
import jax.numpy as jnp
from jax import lax
from jax.experimental import pallas as pl
from jax.experimental.pallas import tpu as pltpu
from jax.sharding import Mesh, PartitionSpec as P

ALL_AXES = ("dp", "xh", "z", "y", "c")
RING = 4
CORES = 2
CAP = 4
TOP = 8
GROUP = 16
META = 128
HALF = 3584
BLOCK = 128
SHIFTS = (0, 1, 3, 2)
ROUTE = (("y", "y"), ("z", "x"), ("x", "z"))
SMALL_VMEM = 24 << 20
LARGE_VMEM = 56 << 20
PROJECT_VMEM = 30 << 20
EXPERT_VMEM = 18 << 20


def flat_index(x, z, y, c):
    return ((((x % 2) * 2 + x // 2) * RING + z) * RING + y) * CORES + c


def ring_perm(axes, shift, cross=False):
    pairs = []
    for x, z, y, c in itertools.product(range(RING), range(RING), range(RING), range(CORES)):
        there = {"x": x, "z": z, "y": y}
        there[axes[c]] = (there[axes[c]] + shift) % RING
        target = flat_index(there["x"], there["z"], there["y"], 1 - c if cross else c)
        pairs.append((flat_index(x, z, y, c), target))
    return pairs


def together(*values):
    return lax.optimization_barrier(values)


def back_perm(axes, shift, cross=False):
    return [(target, source) for source, target in ring_perm(axes, shift, cross)]


def gathered(value, axes):
    return [value] + [lax.ppermute(value, ALL_AXES, ring_perm(axes, s)) for s in SHIFTS[1:]]


def scattered(blocks, axes):
    return [blocks[0]] + [lax.ppermute(b, ALL_AXES, back_perm(axes, s)) for b, s in zip(blocks[1:], SHIFTS[1:])]


def other_core(value):
    return lax.ppermute(value, "c", [(0, 1), (1, 0)])


def hop(blocks, axes, perm, numbers, cross=False):
    return [other_core(blocks[r]) if r == 0 else lax.ppermute(blocks[r], ALL_AXES, perm(axes, SHIFTS[r], cross))
            for r in numbers]


def column_chunks(width):
    steps, start = [], 0
    while start < width:
        size = min(1792, width - start)
        steps.append((start, size))
        start += size
    return steps


def iota(shape, dim):
    return lax.broadcasted_iota(jnp.int32, shape, dim)


def slots_of(meta, experts):
    turned = jnp.transpose(meta.astype(jnp.float32))
    owner = turned[:TOP]
    match = [owner == e.astype(jnp.float32) for e in experts]
    hits = [jnp.max(jnp.where(m, 1.0, 0.0), axis=0, keepdims=True) for m in match]
    stacked = jnp.concatenate(hits * (8 // len(hits)), axis=0)
    row, col = iota((BLOCK, BLOCK), 0), iota((BLOCK, BLOCK), 1)
    before = jnp.where((row // GROUP == col // GROUP) & (row < col), 1.0, 0.0)
    rank = jnp.dot(stacked.astype(jnp.bfloat16), before.astype(jnp.bfloat16),
                   preferred_element_type=jnp.float32)
    base = (iota((1, BLOCK), 1) // GROUP * CAP).astype(jnp.float32)
    slot = iota((BLOCK // RING, BLOCK), 0).astype(jnp.float32)
    place = [slot == jnp.where(h > 0.5, base + rank[e:e + 1], -1.0) for e, h in enumerate(hits)]
    return place, match, turned


def experts_at(info):
    own = [info[4 + r] for r in range(RING)]
    return own + [e ^ 1 for e in own]


def pack_kernel(cross, info, *refs):
    blocks, outs = refs[:RING], refs[RING:]
    experts = experts_at(info)[RING * cross:RING * cross + RING]
    rows = BLOCK // RING
    for b in range(RING):
        place, _, _ = slots_of(blocks[b][:, HALF:HALF + META], experts)
        spread = jnp.concatenate([jnp.where(p, 1.0, 0.0) for p in place], axis=0).astype(jnp.bfloat16)
        for start, size in column_chunks(HALF):
            cols = slice(start, start + size)
            got = jnp.dot(spread, blocks[b][:, cols], preferred_element_type=jnp.float32).astype(jnp.bfloat16)
            for e, out in enumerate(outs):
                out[rows * b:rows * (b + 1), cols] = got[rows * e:rows * (e + 1)]


VMEM_SPEC = pl.BlockSpec(memory_space=pltpu.VMEM)
SMEM_SPEC = pl.BlockSpec(memory_space=pltpu.SMEM)
HBM_SPEC = pl.BlockSpec(memory_space=pltpu.HBM)


def pack(info, blocks, cross):
    return list(pl.pallas_call(
        functools.partial(pack_kernel, cross),
        out_shape=[jax.ShapeDtypeStruct((BLOCK, HALF), jnp.bfloat16)] * RING,
        in_specs=[SMEM_SPEC] + [VMEM_SPEC] * RING,
        out_specs=[VMEM_SPEC] * RING,
        compiler_params=pltpu.CompilerParams(vmem_limit_bytes=SMALL_VMEM),
        cost_estimate=pl.CostEstimate(
            flops=2 * RING * BLOCK * BLOCK * HALF, bytes_accessed=16 * BLOCK * HALF, transcendentals=0),
    )(info, *blocks))


def mixer_of(info, meta):
    place, match, turned = slots_of(meta, experts_at(info))
    parts = []
    for offset in (TOP, 2 * TOP):
        mix = turned[offset:offset + TOP]
        picked = [jnp.sum(jnp.where(m, mix, 0.0), axis=0, keepdims=True) for m in match]
        weight = jnp.concatenate([jnp.where(p, w, 0.0) for p, w in zip(place, picked)], axis=0)
        parts.append(jnp.transpose(weight))
    return jnp.concatenate(parts, axis=0).astype(jnp.bfloat16)


def combine_kernel(mixers, *refs):
    blocks, outs = refs[:2 * RING], refs[2 * RING:]
    rows = BLOCK // RING
    for b in range(RING):
        mixer = mixers[2 * BLOCK * b:2 * BLOCK * (b + 1)]
        for start, size in column_chunks(HALF):
            cols = slice(start, start + size)
            data = jnp.concatenate([block[rows * b:rows * (b + 1), cols] for block in blocks], axis=0)
            got = jnp.dot(mixer, data, preferred_element_type=jnp.float32)
            outs[b][:, cols] = (got[:BLOCK] + got[BLOCK:]).astype(jnp.bfloat16)


def combine(mixers, blocks):
    return list(pl.pallas_call(
        combine_kernel,
        out_shape=[jax.ShapeDtypeStruct((BLOCK, HALF), jnp.bfloat16)] * RING,
        in_specs=[VMEM_SPEC] * (1 + 2 * RING),
        out_specs=[VMEM_SPEC] * RING,
        compiler_params=pltpu.CompilerParams(vmem_limit_bytes=SMALL_VMEM),
        cost_estimate=pl.CostEstimate(
            flops=8 * RING * BLOCK * BLOCK * HALF, bytes_accessed=24 * BLOCK * HALF, transcendentals=0),
    )(mixers, *blocks))


def weight_copies(chunks, gate_hbm, up_hbm, w_in, in_sem):
    half = w_in.shape[1] // 2
    copies, at = [], 0
    for i, (col, size) in enumerate(chunks):
        col = pl.multiple_of(col, BLOCK)
        copies.append((
            pltpu.make_async_copy(gate_hbm.at[pl.ds(col, size)], w_in.at[pl.ds(at, size), pl.ds(0, half)],
                                  in_sem.at[2 * i]),
            pltpu.make_async_copy(up_hbm.at[pl.ds(col, size)], w_in.at[pl.ds(at, size), pl.ds(half, half)],
                                  in_sem.at[2 * i + 1])))
        at += size
    return copies


def block_copies(blocks, target, sems, first):
    return [pltpu.make_async_copy(blocks[r], target.at[pl.ds(r * BLOCK, BLOCK)], sems.at[first + r])
            for r in range(RING)]


def start_all(copies):
    for copy in copies:
        copy.start()


def wait_all(copies):
    for copy in copies:
        copy.wait()


def begin_kernel(info, pairs, tokens, picks, mix, mine, theirs):
    slot = picks[...]
    moved = slot < 0
    for i in range(pairs.shape[0]):
        for j in range(pairs.shape[1]):
            moved = moved | (slot == pairs[i, j])
    owner = jnp.where(moved, slot ^ 32, slot).astype(jnp.bfloat16)
    high = mix[...].astype(jnp.bfloat16)
    low = (mix[...] - high.astype(jnp.float32)).astype(jnp.bfloat16)
    meta = jnp.zeros((GROUP, META), jnp.float32)
    for i, part in enumerate((owner, high, low)):
        lane = iota((TOP, META), 1) == iota((TOP, META), 0) + i * TOP
        lane = jnp.where(lane, 1.0, 0.0).astype(jnp.bfloat16)
        meta += lax.dot_general(part, lane, (((0,), (0,)), ((), ())), preferred_element_type=jnp.float32)
    meta = meta.astype(jnp.bfloat16)
    mine[:, HALF:] = meta
    theirs[:, HALF:] = meta
    for core in range(CORES):
        @pl.when(info[0] == core)
        def _():
            mine[:, :HALF] = tokens[:, HALF * core:HALF * (core + 1)]
            theirs[:, :HALF] = tokens[:, HALF * (1 - core):HALF * (2 - core)]


def begin(info, pairs, tokens, picks, mix):
    out = jax.ShapeDtypeStruct((GROUP, HALF + META), jnp.bfloat16)
    return pl.pallas_call(
        begin_kernel,
        out_shape=[out, out],
        in_specs=[SMEM_SPEC, SMEM_SPEC] + [VMEM_SPEC] * 3,
        out_specs=[VMEM_SPEC, VMEM_SPEC],
        compiler_params=pltpu.CompilerParams(vmem_limit_bytes=SMALL_VMEM),
    )(info, pairs.T, tokens, picks.T, mix.T)


def project_kernel(info, *refs):
    blocks, (gate_hbm, up_hbm, down_hbm), (total, w_far, w_out) = refs[:RING], refs[RING:RING + 3], refs[RING + 3:RING + 6]
    x, w_in, x_sem, in_sem, far_sem, down_sem = refs[RING + 6:]
    at_near, at_far = info[0] * HALF, (1 - info[0]) * HALF
    steps = column_chunks(HALF)
    x_copies = block_copies(blocks, x, x_sem, 0)
    in_copies = weight_copies([(at_near + start, size) for start, size in steps], gate_hbm, up_hbm, w_in, in_sem)
    far_copies = weight_copies([(at_far, HALF)], gate_hbm, up_hbm, w_far, far_sem)[0]
    down_copy = pltpu.make_async_copy(
        down_hbm.at[:, pl.ds(pl.multiple_of(at_near, BLOCK), HALF)], w_out, down_sem)
    start_all(x_copies)
    for pair in in_copies:
        start_all(pair)
    start_all(far_copies)
    down_copy.start()
    wait_all(x_copies)
    for (start, size), pair in zip(steps, in_copies):
        wait_all(pair)
        cols = slice(start, start + size)
        got = jnp.dot(x[:, cols], w_in[cols, :], preferred_element_type=jnp.float32)
        if start == 0:
            total[...] = got
        else:
            total[...] += got
    wait_all(far_copies)
    down_copy.wait()


def project(info, blocks, gate_w, up_w, down_w):
    rows, hid = RING * BLOCK, gate_w.shape[1]
    bf = jnp.bfloat16
    return pl.pallas_call(
        project_kernel,
        out_shape=[jax.ShapeDtypeStruct((rows, 2 * hid), jnp.float32),
                   jax.ShapeDtypeStruct((HALF, 2 * hid), bf), jax.ShapeDtypeStruct((hid, HALF), bf)],
        in_specs=[SMEM_SPEC] + [HBM_SPEC] * 7,
        out_specs=[VMEM_SPEC] * 3,
        scratch_shapes=[
            pltpu.VMEM((rows, HALF), bf), pltpu.VMEM((HALF, 2 * hid), bf),
            pltpu.SemaphoreType.DMA((RING,)), pltpu.SemaphoreType.DMA((2 * len(column_chunks(HALF)),)),
            pltpu.SemaphoreType.DMA((2,)), pltpu.SemaphoreType.DMA,
        ],
        compiler_params=pltpu.CompilerParams(vmem_limit_bytes=PROJECT_VMEM),
        cost_estimate=pl.CostEstimate(
            flops=4 * rows * HALF * hid, bytes_accessed=2 * (5 * HALF * hid + rows * HALF), transcendentals=0),
    )(info, *blocks, gate_w, up_w, down_w)


def expert_kernel(info, near, w_in, w_out, *refs):
    far, main_outs, hidden_far = refs[:RING], refs[RING:2 * RING], refs[2 * RING]
    x, a2, h1, h2, o, x_sem, out_sem = refs[2 * RING + 1:]
    first = info[0] == 0
    half = w_in.shape[1] // 2
    steps = column_chunks(HALF)
    far_copies = [
        [pltpu.make_async_copy(
            far[r].at[:, pl.ds(start, size)], x.at[pl.ds(r * BLOCK, BLOCK), pl.ds(start, size)],
            x_sem.at[RING * i + r]) for r in range(RING)]
        for i, (start, size) in enumerate(steps)]
    for copies in far_copies:
        start_all(copies)
    for (start, size), copies in zip(steps, far_copies):
        wait_all(copies)
        cols = slice(start, start + size)
        got = jnp.dot(x[:, cols], w_in[cols, :], preferred_element_type=jnp.float32)
        if start == 0:
            a2[...] = got
        else:
            a2[...] += got

    rows = BLOCK // RING

    def activate(i, carry):
        left, right = i, i % RING * RING + i // RING
        i1 = pl.multiple_of(jnp.where(first, left, right) * rows, rows)
        i2 = pl.multiple_of(jnp.where(first, right, left) * rows, rows)
        both = near[pl.ds(i1, rows)] + a2[pl.ds(i2, rows)]
        gate, up = both[:, :half], both[:, half:]
        value = gate / (1.0 + jnp.exp(-gate)) * up
        h1[pl.ds(i1, rows)] = value
        h2[pl.ds(i2, rows)] = value
        return carry

    lax.fori_loop(0, RING ** 2, activate, 0)
    hidden_far[...] = h2[...].astype(jnp.bfloat16)
    hidden = h1[...].astype(jnp.bfloat16)
    out_copies = []
    for i, (start, size) in enumerate(steps):
        got = jnp.dot(hidden, w_out[:, start:start + size], preferred_element_type=jnp.float32)
        o[:, start:start + size] = got.astype(jnp.bfloat16)
        for r in range(RING):
            out_copies.append(pltpu.make_async_copy(
                o.at[pl.ds(r * BLOCK, BLOCK), pl.ds(start, size)],
                main_outs[r].at[:, pl.ds(start, size)], out_sem.at[RING * i + r]))
            out_copies[-1].start()
    wait_all(out_copies)


def expert(info, near, w_in, w_out, far):
    rows, hid = RING * BLOCK, w_out.shape[0]
    steps = len(column_chunks(HALF))
    bf, f32 = jnp.bfloat16, jnp.float32
    out = pl.pallas_call(
        expert_kernel,
        out_shape=[jax.ShapeDtypeStruct((BLOCK, HALF), bf)] * RING + [jax.ShapeDtypeStruct((rows, hid), bf)],
        in_specs=[SMEM_SPEC] + [VMEM_SPEC] * 3 + [HBM_SPEC] * RING,
        out_specs=[HBM_SPEC] * RING + [VMEM_SPEC],
        scratch_shapes=[
            pltpu.VMEM((rows, HALF), bf), pltpu.VMEM((rows, 2 * hid), f32),
            pltpu.VMEM((rows, hid), f32), pltpu.VMEM((rows, hid), f32), pltpu.VMEM((rows, HALF), bf),
            pltpu.SemaphoreType.DMA((RING * steps,)), pltpu.SemaphoreType.DMA((RING * steps,)),
        ],
        compiler_params=pltpu.CompilerParams(vmem_limit_bytes=EXPERT_VMEM),
        cost_estimate=pl.CostEstimate(
            flops=6 * rows * HALF * hid, bytes_accessed=4 * rows * HALF, transcendentals=rows * hid),
    )(info, near, w_in, w_out, *far)
    return list(out[:RING]), out[RING]


def spread_kernel(info, hidden, down_hbm, *refs):
    metas, outs, (mixers, w_out, down_sem) = refs[:RING], refs[RING:2 * RING], refs[2 * RING:]
    base = (1 - info[0]) * HALF
    steps = column_chunks(HALF)
    copies = [pltpu.make_async_copy(
        down_hbm.at[:, pl.ds(pl.multiple_of(base + start, BLOCK), size)], w_out.at[:, pl.ds(start, size)],
        down_sem.at[i]) for i, (start, size) in enumerate(steps)]
    start_all(copies)
    for b in range(RING):
        mixers[2 * BLOCK * b:2 * BLOCK * (b + 1)] = mixer_of(info, metas[b][...])
    for (start, size), copy in zip(steps, copies):
        copy.wait()
        cols = slice(start, start + size)
        got = jnp.dot(hidden[...], w_out[:, cols], preferred_element_type=jnp.float32).astype(jnp.bfloat16)
        for r in range(RING):
            outs[r][:, cols] = got[BLOCK * r:BLOCK * (r + 1)]


def spread(info, hidden, down_w, pool):
    rows, hid = hidden.shape
    meta_spec = pl.BlockSpec((BLOCK, META), lambda i: (0, HALF // META))
    out = pl.pallas_call(
        spread_kernel,
        grid=(1,),
        out_shape=[jax.ShapeDtypeStruct((BLOCK, HALF), jnp.bfloat16)] * RING + [
            jax.ShapeDtypeStruct((2 * BLOCK * RING, 2 * BLOCK), jnp.bfloat16)],
        in_specs=[SMEM_SPEC, VMEM_SPEC, HBM_SPEC] + [meta_spec] * RING,
        out_specs=[VMEM_SPEC] * (RING + 1),
        scratch_shapes=[
            pltpu.VMEM((hid, HALF), jnp.bfloat16), pltpu.SemaphoreType.DMA((len(column_chunks(HALF)),))],
        compiler_params=pltpu.CompilerParams(vmem_limit_bytes=LARGE_VMEM),
        cost_estimate=pl.CostEstimate(
            flops=2 * rows * HALF * hid, bytes_accessed=2 * HALF * (hid + rows), transcendentals=0),
    )(info, hidden, down_w, *pool)
    return list(out[:RING]), out[RING]


def summed(blocks):
    return sum(b.astype(jnp.float32) for b in blocks).astype(jnp.bfloat16)


def split_rows(value):
    return list(value.reshape(RING, -1, value.shape[-1]))


def per_device(tokens, picks, mix_weights, pairs, gate_weight, up_weight, down_weight):
    tok_rows, width = tokens.shape
    c = lax.axis_index("c")
    x = lax.axis_index("xh") * 2 + lax.axis_index("dp")
    z = lax.axis_index("z")
    y = lax.axis_index("y")
    first = c == 0

    shifts = jnp.array(SHIFTS, jnp.int32)
    place = lambda x, z, y: ((x // 2 * RING + z) * RING + y) * CORES + c + 0 * shifts
    along_x = place((x + shifts) % RING, z, y)
    along_z = place(x, (z + shifts) % RING, y)
    info = jnp.concatenate([jnp.stack([c, c, c, c]), jnp.where(first, along_x, along_z)]).astype(jnp.int32)

    mine, theirs = begin(info, pairs, tokens, picks, mix_weights)
    theirs = other_core(theirs)
    pool = jnp.where(first, jnp.concatenate([mine, theirs]), jnp.concatenate([theirs, mine]))
    part, line = together(lax.ppermute(pool, ALL_AXES, ring_perm(ROUTE[1], SHIFTS[3])), gathered(pool, ROUTE[0]))
    line = jnp.concatenate(line, axis=0)
    ahead, part = together(hop([line] * RING, ROUTE[1], ring_perm, (1, 2)), gathered(part, ROUTE[0]))
    pool = [line] + ahead + [jnp.concatenate(part, axis=0)]

    own, far = pack(info, pool, 0), pack(info, pool, 1)
    own = own[:1] + hop(own, ROUTE[2], ring_perm, (1, 2, 3))
    far = hop(far, ROUTE[2], ring_perm, (0, 1, 2, 3), cross=True)
    gate_w, up_w, down_w = gate_weight[0], up_weight[0], down_weight[0]
    near, w_in, w_out = project(info, own, gate_w, up_w, down_w)
    own, hidden = expert(info, near, w_in, w_out, far)
    far, mixers = spread(info, hidden, down_w, pool)
    own = own[:1] + hop(own, ROUTE[2], back_perm, (1, 2, 3))
    far = hop(far, ROUTE[2], back_perm, (0, 1, 2, 3), cross=True)
    sums = combine(mixers, own + far)
    ahead, part = together(hop(sums, ROUTE[1], back_perm, (1, 2)), scattered(split_rows(sums[3]), ROUTE[0]))
    line, part = summed(sums[:1] + ahead), summed(part)
    part, line = together(
        lax.ppermute(part, ALL_AXES, back_perm(ROUTE[1], SHIFTS[3])), scattered(split_rows(line), ROUTE[0]))
    done = summed(line + [part])
    own = jnp.where(first, done[:tok_rows], done[tok_rows:])
    rest = other_core(jnp.where(first, done[tok_rows:], done[:tok_rows]))
    return jnp.where(first, jnp.concatenate([own, rest], axis=1), jnp.concatenate([rest, own], axis=1))


def solution(mesh):
    fine = Mesh(mesh.devices.reshape(2, 2, RING, RING, CORES), ALL_AXES)
    experts = ("xh", "z", "y", "c")
    return jax.shard_map(
        per_device,
        mesh=fine,
        in_specs=(
            P(ALL_AXES, None),
            P(ALL_AXES, None),
            P(ALL_AXES, None),
            P(),
            P(experts, None, "dp"),
            P(experts, None, "dp"),
            P(experts, "dp", None),
        ),
        out_specs=P(ALL_AXES, None),
        check_vma=False,
    )
```
